512 devices in a mesh: occ: 8 (over x_lo, y), vir: 64 (over z, x_hi, core).
Axes of the slice: x: 4 (x_hi: 2, x_lo: 2; x = x_hi * 2 + x_lo), y: 4, z: 16, core: 2. Of those that a mesh axis runs over, the one named last changes fastest.
Arguments:
- amplitudes: float32 [1600, 230400], P('occ', 'vir'), may hold values from -6 to 6
- singles: float32 [40, 480], replicated, may hold values from -3 to 3
- integrals: float32 [2, 230400, 256], P(None, 'vir', 'occ'), may hold values from -0.1875 to 0.1875
- occ_irrep: int32 [40], replicated, may hold values from 0 to 7, never falling along the last dimension, each value on 1 to 10 neighbouring positions
- vir_irrep: int32 [480], replicated, may hold values from 0 to 7, never falling along the last dimension, each value on 1 to 120 neighbouring positions
- owner: int32 [64], replicated, may hold values from 0 to 63, each once
Outputs:
- residual: float32 [1600, 512], P('occ', 'vir')
The draws below stay inside these ranges and needn't reach their ends.
Inputs may be any that keep to these rules, and one draw needn't show every extreme that they name: `occ_irrep`: labels never fall from one orbital to the next; each of the 8 irreps holds between 1 and 10 orbitals, one exactly that many. `vir_irrep`: labels never fall from one orbital to the next; each of the 8 irreps holds between 1 and 120 orbitals, one exactly that many. `owner`: every vir index owns exactly one block.
All inputs are finite; a program needn't handle non-finite values.
Results may differ from the reference program's by a relative error of at most 0.0003.
Values sent between devices are 32-bit elements; how exact they have to be, the bound alone decides.
No kernel may reach another device: no remote copies, remote signals or barrier semaphores. Data moves between devices by JAX's collectives and lax.ppermute only.
A program may use at most 64 MiB of HBM per device.

```python
import math
import jax
import jax.numpy as jnp
import numpy as np
from jax import lax

NO = 40
NV = 480
SPAN = 256
IJ = 1600
CD = 230400
BW = 4
N_VIR = 64


def with_spikes(drawn, own_key, source, target, blocks, factor):
    def block_of(position):
        return (jnp.arange(drawn.shape[position]) // (drawn.shape[position] // blocks)).reshape((-1,) + (1,) * (drawn.ndim - 1 - position))

    near = jax.random.permutation(own_key, blocks)[block_of(target)]
    second = (block_of(target) + blocks // 2) % blocks
    return jnp.where((block_of(source) == near) | (block_of(source) == second), factor * drawn, drawn)


def block_scale(key, extent, pieces, least, high):
    gain, own = 1.0, jax.random.fold_in(key, 6)
    for axis_at, parts in pieces:
        heights = jnp.exp(jax.random.uniform(jax.random.fold_in(own, axis_at), (parts,), jnp.float32, least / len(pieces), high / len(pieces)))
        gain = gain * jnp.repeat(heights, extent[axis_at] // parts).reshape([-1 if axis == axis_at else 1 for axis in range(len(extent))])
    return gain


def length_profile(number_of, total, bound, slope):
    weights = [(1 << 20) // math.isqrt(rank ** slope) + 1 for rank in range(2, number_of + 1)]
    rest, holding = total - bound - (number_of - 1), [1] * (number_of - 1)
    while rest > 0:
        movable = [i for i in range(number_of - 1) if holding[i] < bound]
        whole, remaining = sum([weights[i] for i in movable]), rest
        for i in movable:
            more = min(bound - holding[i], max(1, remaining * weights[i] // whole), rest)
            holding[i] = holding[i] + more
            rest = rest - more
    return np.array([bound] + holding)


def ragged_sizes(stream_key, amount, total, most, lean):
    if amount == 2:
        one = jax.random.randint(stream_key, (), max(1, total - most), min(most, total - 1) + 1)
        return jnp.stack([one, total - one])
    sizes = jnp.asarray(length_profile(amount, total, most, lean), jnp.int32)
    pairs = (amount - 1) // 2
    source_of, taker = sizes[1:1 + 2 * pairs:2], sizes[2:2 + 2 * pairs:2]
    margin = jnp.minimum(source_of - 1, most - taker)
    moved = jax.random.randint(jax.random.fold_in(stream_key, 1), (pairs,), 0, 1 << 20) % (margin + 1)
    sizes = sizes.at[1:1 + 2 * pairs:2].set(source_of - moved).at[2:2 + 2 * pairs:2].set(taker + moved)
    return sizes[jax.random.permutation(jax.random.fold_in(stream_key, 2), amount)]


def centred(key, dims, scale, limit, split=(), kind=jnp.bfloat16):
    array = scale * jax.random.normal(key, dims, jnp.float32)
    if split:
        array = array * block_scale(key, dims, split, -0.22, 0.18)
    return jnp.clip(array, -limit, limit).astype(kind)


def heavy_noise(rng, shape, spread, bound, pieces, heavy, held_as=jnp.bfloat16):
    array = spread * jax.random.normal(rng, shape, jnp.float32)
    if pieces:
        array = array * block_scale(rng, shape, pieces, -0.22, 0.18)
    return jnp.clip(with_spikes(array, jax.random.fold_in(rng, 3), *heavy), -bound, bound).astype(held_as)


def setup_inputs(seed: int = 0) -> dict:
    key_of = jax.random.split(jax.random.key(seed), 7)
    return {
        "amplitudes": centred(key_of[0], (IJ, CD), 1.0, 6.0, ((0, 8), (1, 64)), jnp.float32),
        "singles": centred(key_of[1], (NO, NV), 0.5, 3.0, (), jnp.float32),
        "integrals": heavy_noise(key_of[2], (2, CD, SPAN), (CD // 32) ** -0.5, 0.1875, ((1, 64), (2, 8)), (1, 2, 64, 4.0), jnp.float32),
        "occ_irrep": jnp.searchsorted(jnp.cumsum(ragged_sizes(key_of[3], 8, NO, NO // 4, 0)), jnp.arange(NO), side="right").astype(jnp.int32),
        "vir_irrep": jnp.searchsorted(jnp.cumsum(ragged_sizes(key_of[4], 8, NV, NV // 4, 1)), jnp.arange(NV), side="right").astype(jnp.int32),
        "owner": jax.random.permutation(key_of[5], N_VIR).astype(jnp.int32),
    }


def reference(amplitudes, singles, integrals, occ_irrep, vir_irrep, owner):
    singles_sym = jnp.where(occ_irrep[:, None] == vir_irrep[None, :], singles, jnp.float32(0.0))
    sym_cd = jnp.bitwise_xor(vir_irrep[:, None], vir_irrep[None, :]).reshape(NV * NV)
    pair_index = jnp.arange(2 * SPAN, dtype=jnp.int32)
    first_orbital = pair_index // NV
    second_orbital = pair_index % NV
    sym_ab = jnp.bitwise_xor(vir_irrep[first_orbital], vir_irrep[second_orbital]).reshape(2, SPAN)
    blocks = amplitudes.reshape(NO, NO, NV * NV)

    def one_row(inputs):
        amp_row, single_row, irrep_row = inputs
        product = (single_row[None, :, None] * singles_sym[:, None, :]).reshape(NO, NV * NV)
        sym_ij = jnp.bitwise_xor(irrep_row, occ_irrep)
        tau_rows = jnp.where(sym_ij[:, None] == sym_cd[None, :], amp_row + product, jnp.float32(0.0))
        ladder = 0.5 * jnp.einsum("jc,hcn->hjn", tau_rows, integrals, precision=lax.Precision.HIGHEST)
        keep = sym_ij[None, :, None] == sym_ab[:, None, :]
        return jnp.where(keep, ladder, jnp.float32(0.0))

    ladder_all = lax.map(one_row, (blocks, singles_sym, occ_irrep))
    ladder_all = jnp.transpose(ladder_all, (1, 0, 2, 3)).reshape(2, NO * NO, SPAN)
    block_ids = jnp.arange(N_VIR, dtype=jnp.int32)
    matches = owner[:, None] == block_ids[None, :]
    inverse = jnp.sum(jnp.where(matches, block_ids[:, None], 0), axis=0).astype(jnp.int32)
    grouped = ladder_all.reshape(2, NO * NO, N_VIR, BW)
    ordered = jnp.take(grouped, inverse, axis=2)
    return jnp.transpose(ordered, (1, 2, 0, 3)).reshape(NO * NO, 2 * SPAN)
```

```python
import functools

import jax
import jax.numpy as jnp
from jax import lax
from jax.experimental import pallas as pl
from jax.experimental.pallas import tpu as pltpu
from jax.sharding import PartitionSpec as P

NO = 40
NV = 480
SPAN = 256
IRREPS = 8
RUN_V = 120
RUN_O = 10
ROWS_I = 5
COLS = 32
CD = 3600
SLOTS = 8
LEAD = 256
WIDE = 33 * 128
MAIN = 28 * 128
GROUP = 64
PACK = 2 * SLOTS * RUN_V
VMEM = 32 * 1024 * 1024


def placed():
    return lax.axis_index("occ"), lax.axis_index("vir")


def fill_starts(labels, length, starts):
    top = 1
    while top * 2 <= length:
        top *= 2
    starts[0] = jnp.int32(0)
    starts[IRREPS] = jnp.int32(length)
    for g in range(1, IRREPS):
        low = jnp.int32(0)
        bit = top
        while bit:
            cand = low + bit
            below = labels[jnp.minimum(cand, length) - 1] < g
            low = jnp.where((cand <= length) & below, cand, low)
            bit //= 2
        starts[g] = low


def irrep_of(index, starts):
    total = jnp.zeros_like(index)
    for g in range(1, IRREPS):
        total += (index >= starts[g]).astype(jnp.int32)
    return total


def join(near, far, position):
    shift = lax.rem(position, 128)
    back = lax.rem(128 - shift, 128)
    lanes = lax.broadcasted_iota(jnp.int32, near.shape, 1)
    return jnp.where(
        lanes < 128 - shift, pltpu.roll(near, back, axis=1), pltpu.roll(far, back, axis=1)
    )


def window(ref, lead, position):
    base = pl.multiple_of((position // 128) * 128, 128)
    near = ref[lead + (pl.ds(base, 128),)]
    far = ref[lead + (pl.ds(base + 128, 128),)]
    return join(near, far, position)


def tile_window(ref, rows, position):
    tile = position // 128
    return join(ref[tile, rows, :], ref[tile + 1, rows, :], position)


def place_slot(ref, rows, slot, value, lanes):
    tile, inner = divmod(slot * RUN_V, 128)
    if inner == 0:
        ref[rows, pl.ds(tile * 128, 128)] = value
        return
    turned = pltpu.roll(value, inner, axis=1)
    old = ref[rows, pl.ds(tile * 128, 128)]
    ref[rows, pl.ds(tile * 128, 128)] = jnp.where(lanes >= inner, turned, old)
    if slot == SLOTS - 1:
        turned = jnp.where(lanes < SLOTS * RUN_V - (tile + 1) * 128, turned, 0.0)
    ref[rows, pl.ds((tile + 1) * 128, 128)] = turned


def pack_kernel(
    where_am_i,
    vir_ref,
    occ_ref,
    amp_hbm,
    amp_tail,
    int_hbm,
    int_tail,
    singles_ref,
    packed_ref,
    high_ref,
    low_ref,
    vstart,
    ostart,
    ints,
    amps,
    chunk,
    group,
    ones,
    single_win,
    left,
    sems,
):
    int_copy = pltpu.make_async_copy(
        int_hbm.at[:, :, pl.ds(0, MAIN)], ints.at[:, :, pl.ds(LEAD, MAIN)], sems.at[0]
    )
    amp_copies = [
        pltpu.make_async_copy(
            amp_hbm.at[:, pl.ds(t * 128, 128)],
            amps.at[LEAD // 128 + t, pl.ds(0, ROWS_I * NO), :],
            sems.at[1 + t],
        )
        for t in range(MAIN // 128)
    ]
    int_copy.start()
    for copy in amp_copies:
        copy.start()
    o, v = where_am_i()
    fill_starts(vir_ref, NV, vstart)
    fill_starts(occ_ref, NO, ostart)
    c_first = (v * 15) // 2
    offset = (v % 2) * (NV // 2)

    tail = CD - MAIN
    ints[:, :, pl.ds(0, LEAD)] = jnp.zeros((2, COLS, LEAD), jnp.float32)
    lanes3 = lax.broadcasted_iota(jnp.int32, (2, COLS, 128), 2)
    ints[:, :, pl.ds(LEAD + MAIN, 128)] = jnp.where(lanes3 < tail, int_tail[...], 0.0)
    rest = WIDE - LEAD - MAIN - 128
    ints[:, :, pl.ds(LEAD + MAIN + 128, rest)] = jnp.zeros((2, COLS, rest), jnp.float32)
    amps[(LEAD + MAIN) // 128, pl.ds(0, ROWS_I * NO), :] = amp_tail[...]
    amps[:, pl.ds(ROWS_I * NO, 16), :] = jnp.zeros((WIDE // 128, 16, 128), jnp.float32)

    int_copy.wait()
    lanes = lax.broadcasted_iota(jnp.int32, (COLS, 128), 1)
    row = lax.broadcasted_iota(jnp.int32, (COLS, 128), 0)
    for s in range(2):
        first = s * SPAN + o * COLS
        a = (first >= NV).astype(jnp.int32)
        b = first - a * NV
        irr_a = vir_ref[a]
        irr_b = irrep_of(row + b, vstart)
        low_h = vir_ref[b]
        high_h = vir_ref[b + COLS - 1]
        for slot in range(SLOTS):
            irr_c = vir_ref[c_first + slot]
            turn = irr_c ^ irr_a

            def one(h, value, slot=slot, turn=turn, irr_b=irr_b, s=s):
                position = LEAD + slot * NV + vstart[turn ^ h] - offset
                return jnp.where(irr_b == h, window(ints, (s, slice(None)), position), value)

            value = lax.fori_loop(low_h, high_h + 1, one, jnp.zeros((COLS, 128), jnp.float32))
            place_slot(chunk.at[s], pl.ds(0, COLS), slot, value, lanes)
    full = 7 * 128
    packed_ref[:, pl.ds(0, full)] = chunk[0, :, pl.ds(0, full)]
    packed_ref[:, pl.ds(full, 128)] = jnp.where(
        lanes < 64,
        chunk[0, :, pl.ds(full, 128)],
        pltpu.roll(chunk[1, :, pl.ds(full, 128)], 64, axis=1),
    )
    packed_ref[:, pl.ds(full + 128, full)] = chunk[1, :, pl.ds(0, full)]

    ones[...] = jnp.zeros_like(ones)
    for t in range(4):
        size = min(128, NV - t * 128)
        ones[t, pl.ds(0, NO), pl.ds(0, size)] = singles_ref[:, pl.ds(t * 128, size)]
    for g in range(IRREPS):
        single_win[g] = tile_window(ones, pl.ds(ostart[g], 16), vstart[g])
    lane_c = lax.broadcasted_iota(jnp.int32, (8, 128), 1)
    row_i = lax.broadcasted_iota(jnp.int32, (8, 1), 0)
    irr_i = [occ_ref[o * ROWS_I + i] for i in range(ROWS_I)]
    for slot in range(SLOTS):
        c = c_first + slot
        irr_c = vir_ref[c]
        own = ones[c // 128, pl.ds(o * ROWS_I, 8), :]
        column = jnp.sum(jnp.where(lane_c == lax.rem(c, 128), own, 0.0), axis=1, keepdims=True)
        for i in range(ROWS_I):
            column = jnp.where((row_i == i) & (irr_i[i] != irr_c), 0.0, column)
        left[slot] = jnp.broadcast_to(column, (8, 128))

    for copy in amp_copies:
        copy.wait()
    lanes_o = lax.broadcasted_iota(jnp.int32, (RUN_O, 128), 1)
    group[...] = jnp.zeros_like(group)

    def symmetry(sym, carry):
        for slot in range(SLOTS):
            g = vir_ref[c_first + slot] ^ sym
            begin = slot * NV + vstart[g] - offset
            from_lane = jnp.maximum(0, -begin)
            to_lane = jnp.minimum(vstart[g + 1] - vstart[g], CD - begin)
            keep = (lanes_o >= from_lane) & (lanes_o < to_lane)
            for i in range(ROWS_I):
                j_rows = pl.ds(i * NO + ostart[irr_i[i] ^ sym], RUN_O)
                value = tile_window(amps, j_rows, LEAD + begin)
                product = left[slot, pl.ds(i, 1), :] * single_win[g, pl.ds(0, RUN_O), :]
                value = jnp.where(keep, value + product, 0.0)
                place_slot(group, pl.ds(i * RUN_O, RUN_O), slot, value, lanes_o)
        whole = group[...]
        top = whole.astype(jnp.bfloat16)
        out = pl.ds(pl.multiple_of(sym * GROUP, GROUP), GROUP)
        high_ref[out, :] = top
        low_ref[out, :] = (whole - top.astype(jnp.float32)).astype(jnp.bfloat16)
        return carry

    lax.fori_loop(0, IRREPS, symmetry, 0)


def pack(where_am_i, amplitudes, singles, integrals_t, occ_irrep, vir_irrep):
    depth = SLOTS * 128
    smem = pl.BlockSpec(memory_space=pltpu.SMEM)
    vmem = pl.BlockSpec(memory_space=pltpu.VMEM)
    return pl.pallas_call(
        functools.partial(pack_kernel, where_am_i),
        grid=(1,),
        in_specs=[
            smem,
            smem,
            pl.BlockSpec(memory_space=pl.ANY),
            pl.BlockSpec((ROWS_I * NO, 128), lambda n: (0, MAIN // 128)),
            pl.BlockSpec(memory_space=pl.ANY),
            pl.BlockSpec((2, COLS, 128), lambda n: (0, 0, MAIN // 128)),
            vmem,
        ],
        out_specs=[vmem, vmem, vmem],
        out_shape=[
            jax.ShapeDtypeStruct((COLS, PACK), jnp.float32),
            jax.ShapeDtypeStruct((IRREPS * GROUP, depth), jnp.bfloat16),
            jax.ShapeDtypeStruct((IRREPS * GROUP, depth), jnp.bfloat16),
        ],
        scratch_shapes=[
            pltpu.SMEM((IRREPS + 1,), jnp.int32),
            pltpu.SMEM((IRREPS + 1,), jnp.int32),
            pltpu.VMEM((2, COLS, WIDE), jnp.float32),
            pltpu.VMEM((WIDE // 128, ROWS_I * NO + 16, 128), jnp.float32),
            pltpu.VMEM((2, COLS, depth), jnp.float32),
            pltpu.VMEM((GROUP, depth), jnp.float32),
            pltpu.VMEM((5, NO + 16, 128), jnp.float32),
            pltpu.VMEM((IRREPS, 16, 128), jnp.float32),
            pltpu.VMEM((SLOTS, 8, 128), jnp.float32),
            pltpu.SemaphoreType.DMA((1 + MAIN // 128,)),
        ],
        compiler_params=pltpu.CompilerParams(vmem_limit_bytes=VMEM),
        name="pack",
    )(vir_irrep, occ_irrep, amplitudes, amplitudes, integrals_t, integrals_t, singles)


def ladder_kernel(vir_ref, owner_ref, packed_ref, high_ref, low_ref, out_ref, vstart, top, bottom):
    fill_starts(vir_ref, NV, vstart)
    full = 7 * 128
    for source in range(8):
        for s in range(2):
            wide = packed_ref[source, :, pl.ds(s * (full + 128), full)]
            last = packed_ref[source, :, pl.ds(full, 128)]
            if s == 1:
                last = pltpu.roll(last, 64, axis=1)
            rows = pl.ds(s * SPAN + source * COLS, COLS)
            for part, at, size in ((wide, 0, full), (last, full, 128)):
                upper = part.astype(jnp.bfloat16)
                top[rows, pl.ds(at, size)] = upper
                bottom[rows, pl.ds(at, size)] = (part - upper.astype(jnp.float32)).astype(jnp.bfloat16)
    contract = functools.partial(
        lax.dot_general,
        dimension_numbers=(((1,), (1,)), ((), ())),
        preferred_element_type=jnp.float32,
    )
    upper, lower = top[...], bottom[...]
    high, low = high_ref[...], low_ref[...]
    sums = contract(upper, high) + contract(lower, high) + contract(upper, low)
    column = lax.broadcasted_iota(jnp.int32, (2 * SPAN, 128), 0)
    second = column >= NV
    sym = irrep_of(jnp.where(second, column - NV, column), vstart)
    sym = sym ^ jnp.where(second, vir_ref[1], vir_ref[0])
    pair = sym >> 1
    picked = sums[:, 0:128]
    for t in range(1, 4):
        picked = jnp.where(pair == t, sums[:, t * 128 : (t + 1) * 128], picked)
    span = (column >= SPAN).astype(jnp.int32)
    picked = jnp.where((sym & 1) == span, picked, pltpu.roll(picked, 64, axis=1))
    lanes = lax.broadcasted_iota(jnp.int32, (SPAN, 128), 1)
    both = 0.5 * jnp.where(lanes < 64, picked[:SPAN], picked[SPAN:])
    for k in range(64):
        out_ref[owner_ref[k]] = both[4 * k : 4 * k + 4, :]


def ladder(packed, high, low, vir_irrep, owner):
    smem = pl.BlockSpec(memory_space=pltpu.SMEM)
    vmem = pl.BlockSpec(memory_space=pltpu.VMEM)
    return pl.pallas_call(
        ladder_kernel,
        in_specs=[smem, smem, vmem, vmem, vmem],
        out_specs=vmem,
        out_shape=jax.ShapeDtypeStruct((64, 4, 128), jnp.float32),
        scratch_shapes=[
            pltpu.SMEM((IRREPS + 1,), jnp.int32),
            pltpu.VMEM((2 * SPAN, SLOTS * 128), jnp.bfloat16),
            pltpu.VMEM((2 * SPAN, SLOTS * 128), jnp.bfloat16),
        ],
        compiler_params=pltpu.CompilerParams(vmem_limit_bytes=VMEM),
        name="ladder",
    )(vir_irrep, owner, packed, high, low)


def finish_kernel(where_am_i, vir_ref, occ_ref, owner_ref, parts_ref, out_ref, vstart, ostart):
    o, u = where_am_i()
    fill_starts(vir_ref, NV, vstart)
    fill_starts(occ_ref, NO, ostart)
    block = jnp.int32(0)
    for k in range(64):
        block += jnp.where(owner_ref[k] == u, k, 0)
    total = jnp.sum(parts_ref[...], axis=0)
    both = jnp.concatenate([total, pltpu.roll(total, 64, axis=1)], axis=0)
    wide = jnp.concatenate([both, jnp.zeros_like(both)], axis=1)
    lanes = lax.broadcasted_iota(jnp.int32, (8, 256), 1)
    row = lax.broadcasted_iota(jnp.int32, (8, 256), 0)
    column = jnp.where(row >= 4, SPAN - 4, 0) + block * 4 + row
    second = column >= NV
    sym = irrep_of(jnp.where(second, column - NV, column), vstart)
    sym = sym ^ jnp.where(second, vir_ref[1], vir_ref[0])
    result = jnp.zeros((8, 256), jnp.float32)
    for i in range(ROWS_I):
        mine = sym ^ occ_ref[o * ROWS_I + i]
        for g in range(IRREPS):
            begin = i * NO + ostart[g]
            end = i * NO + ostart[g + 1]
            moved = pltpu.roll(wide, begin - i * RUN_O, axis=1)
            here = (mine == g) & (lanes >= begin) & (lanes < end)
            result = jnp.where(here, moved, result)
    out_ref[...] = result[:, : ROWS_I * NO]


def finish(where_am_i, parts, occ_irrep, vir_irrep, owner):
    smem = pl.BlockSpec(memory_space=pltpu.SMEM)
    vmem = pl.BlockSpec(memory_space=pltpu.VMEM)
    return pl.pallas_call(
        functools.partial(finish_kernel, where_am_i),
        in_specs=[smem, smem, smem, vmem],
        out_specs=vmem,
        out_shape=jax.ShapeDtypeStruct((8, ROWS_I * NO), jnp.float32),
        scratch_shapes=[
            pltpu.SMEM((IRREPS + 1,), jnp.int32),
            pltpu.SMEM((IRREPS + 1,), jnp.int32),
        ],
        name="finish",
    )(vir_irrep, occ_irrep, owner, parts)


def shards(amplitudes, singles, integrals, occ_irrep, vir_irrep, owner):
    turned = jnp.transpose(integrals, (0, 2, 1))
    packed, high, low = pack(placed, amplitudes, singles, turned, occ_irrep, vir_irrep)
    everywhere = jnp.broadcast_to(packed[None], (8,) + packed.shape)
    gathered = lax.all_to_all(everywhere, "occ", 0, 0, tiled=True)
    mine = ladder(gathered, high, low, vir_irrep, owner)
    parts = lax.all_to_all(mine, "vir", 0, 0, tiled=True)
    return jnp.transpose(finish(placed, parts, occ_irrep, vir_irrep, owner))


def solution(mesh):
    specs = (P("occ", "vir"), P(), P(None, "vir", "occ"), P(), P(), P())
    return jax.shard_map(
        shards, mesh=mesh, in_specs=specs, out_specs=P("occ", "vir"), check_vma=False
    )
```

```python
import functools

import jax
import jax.numpy as jnp
from jax import lax
from jax.experimental import pallas as pl
from jax.experimental.pallas import tpu as pltpu
from jax.sharding import PartitionSpec as P

NO = 40
NV = 480
SPAN = 256
IRREPS = 8
RUN_V = 120
RUN_O = 10
ROWS_I = 5
COLS = 32
CD = 3600
SLOTS = 8
LEAD = 256
WIDE = 33 * 128
MAIN = 28 * 128
GROUP = 64
PACK = 2 * SLOTS * RUN_V
ALL_VMEM = 64 * 1024 * 1024
HALF_VMEM = 32 * 1024 * 1024
FULL = 7 * 128
HALF = 64


def placed():
    return lax.axis_index("occ"), lax.axis_index("vir")


def fill_starts(labels, length, starts):
    bit = 1
    while bit * 2 <= length:
        bit *= 2
    low = [jnp.int32(0)] * IRREPS
    while bit:
        for g in range(1, IRREPS):
            cand = low[g] + bit
            below = labels[jnp.minimum(cand, length) - 1] < g
            low[g] = jnp.where((cand <= length) & below, cand, low[g])
        bit //= 2
    for g in range(IRREPS):
        starts[g] = low[g]
    starts[IRREPS] = jnp.int32(length)
    return low


def irrep_of(index, low):
    total = jnp.zeros_like(index)
    for g in range(1, IRREPS):
        total += (index >= low[g]).astype(jnp.int32)
    return total


def turn(near, far, position, inner, lanes):
    shift = lax.rem(position, 128)
    amount = lax.rem(inner + 128 - shift, 128)
    return pltpu.roll(jnp.where(lanes >= shift, near, far), amount, axis=1)


def inner_of(slot):
    return slot * RUN_V % 128


def tiles_of(turned, lanes):
    for slot in range(SLOTS - 1):
        yield jnp.where(lanes < inner_of(slot + 1), turned[slot], turned[slot + 1])
    yield turned[SLOTS - 1]


def first_pair(v):
    return (v * 15) // 2, (v % 2) * (NV // 2)


def pack_kernel(where_am_i, vir_hbm, int_hbm, out_hbm, labels, starts, ints, whole, packed, sems):
    copies = [
        pltpu.make_async_copy(vir_hbm, labels, sems.at[0]),
        pltpu.make_async_copy(
            int_hbm.at[:, :, pl.ds(0, MAIN)], ints.at[:, :, pl.ds(LEAD, MAIN)], sems.at[1]
        ),
        pltpu.make_async_copy(int_hbm, whole, sems.at[2]),
    ]
    for copy in copies:
        copy.start()
    o, v = where_am_i()
    c_first, offset = first_pair(v)
    rest = WIDE - LEAD - MAIN - 128
    ints[:, :, pl.ds(0, LEAD)] = jnp.zeros((2, COLS, LEAD), jnp.float32)
    ints[:, :, pl.ds(LEAD + MAIN, 128)] = jnp.zeros((2, COLS, 128), jnp.float32)
    ints[:, :, pl.ds(LEAD + MAIN + 128, rest)] = jnp.zeros((2, COLS, rest), jnp.float32)
    copies[0].wait()
    low = fill_starts(labels, NV, starts)
    copies[1].wait()
    copies[2].wait()
    ints[:, :, pl.ds(LEAD + MAIN, CD - MAIN)] = whole[:, :, pl.ds(MAIN, CD - MAIN)]

    lanes = lax.broadcasted_iota(jnp.int32, (COLS, 128), 1)
    row = lax.broadcasted_iota(jnp.int32, (COLS, 128), 0)
    sends = []

    def send(at, size):
        for n in range(8):
            copy = pltpu.make_async_copy(
                packed.at[:, pl.ds(at, size)],
                out_hbm.at[n, :, pl.ds(at, size)],
                sems.at[3 + len(sends)],
            )
            copy.start()
            sends.append(copy)

    held = None
    for s in range(2):
        first = s * SPAN + o * COLS
        a = (first >= NV).astype(jnp.int32)
        b = first - a * NV
        irr_a = labels[a]
        irr_b = irrep_of(row + b, low)
        turned = []
        for slot in range(SLOTS):
            cross = labels[c_first + slot] ^ irr_a
            value = jnp.zeros((COLS, 128), jnp.float32)
            for h in range(IRREPS):
                position = LEAD + slot * NV + starts[cross ^ h] - offset
                base = pl.multiple_of((position // 128) * 128, 128)
                near = ints[s, :, pl.ds(base, 128)]
                far = ints[s, :, pl.ds(base + 128, 128)]
                moved = turn(near, far, position, inner_of(slot), lanes)
                value = jnp.where(irr_b == h, moved, value)
            turned.append(value)
        tiles = list(tiles_of(turned, lanes))
        at = s * (FULL + 128)
        for t in range(7):
            packed[:, pl.ds(at + t * 128, 128)] = tiles[t]
        if s == 0:
            held = tiles[7]
            send(0, FULL)
        else:
            packed[:, pl.ds(FULL, 128)] = jnp.where(
                lanes < HALF, held, pltpu.roll(tiles[7], HALF, axis=1)
            )
            send(FULL, FULL + 128)
    for copy in sends:
        copy.wait()


def pack(where_am_i, integrals_t, vir_irrep):
    anywhere = pl.BlockSpec(memory_space=pl.ANY)
    return pl.pallas_call(
        functools.partial(pack_kernel, where_am_i),
        in_specs=[anywhere, anywhere],
        out_specs=anywhere,
        out_shape=jax.ShapeDtypeStruct((8, COLS, PACK), jnp.float32),
        scratch_shapes=[
            pltpu.SMEM((NV,), jnp.int32),
            pltpu.SMEM((IRREPS + 1,), jnp.int32),
            pltpu.VMEM((2, COLS, WIDE), jnp.float32),
            pltpu.VMEM((2, COLS, CD), jnp.float32),
            pltpu.VMEM((COLS, PACK), jnp.float32),
            pltpu.SemaphoreType.DMA((3 + 16,)),
        ],
        compiler_params=pltpu.CompilerParams(vmem_limit_bytes=ALL_VMEM),
        name="pack",
    )(vir_irrep, integrals_t)


def pack_tau(o, v, vir_ref, occ_ref, vstart, ostart, amp_ref, singles_ref, amps, ones, single_win, left, group, high, low):
    c_first, offset = first_pair(v)
    for t in range(CD // 128 + 1):
        size = min(128, CD - t * 128)
        amps[LEAD // 128 + t, pl.ds(0, ROWS_I * NO), pl.ds(0, size)] = amp_ref[:, pl.ds(t * 128, size)]
    amps[:, pl.ds(ROWS_I * NO, 16), :] = jnp.zeros((WIDE // 128, 16, 128), jnp.float32)

    ones[...] = jnp.zeros_like(ones)
    for t in range(4):
        size = min(128, NV - t * 128)
        ones[t, pl.ds(0, NO), pl.ds(0, size)] = singles_ref[:, pl.ds(t * 128, size)]
    lanes_w = lax.broadcasted_iota(jnp.int32, (16, 128), 1)
    for g in range(IRREPS):
        at, rows = vstart[g], pl.ds(ostart[g], 16)
        single_win[g] = turn(ones[at // 128, rows, :], ones[at // 128 + 1, rows, :], at, 0, lanes_w)
    lane_c = lax.broadcasted_iota(jnp.int32, (8, 128), 1)
    row_i = lax.broadcasted_iota(jnp.int32, (8, 1), 0)
    irr_i = [occ_ref[o * ROWS_I + i] for i in range(ROWS_I)]
    for slot in range(SLOTS):
        c = c_first + slot
        irr_c = vir_ref[c]
        own = ones[c // 128, pl.ds(o * ROWS_I, 8), :]
        column = jnp.sum(jnp.where(lane_c == lax.rem(c, 128), own, 0.0), axis=1, keepdims=True)
        for i in range(ROWS_I):
            column = jnp.where((row_i == i) & (irr_i[i] != irr_c), 0.0, column)
        left[slot] = jnp.broadcast_to(column, (8, 128))

    lanes = lax.broadcasted_iota(jnp.int32, (RUN_O, 128), 1)
    group[...] = jnp.zeros_like(group)

    def symmetry(sym, carry):
        turned = [[] for _ in range(ROWS_I)]
        for slot in range(SLOTS):
            g = vir_ref[c_first + slot] ^ sym
            begin = slot * NV + vstart[g] - offset
            from_lane = jnp.maximum(0, -begin)
            to_lane = jnp.minimum(vstart[g + 1] - vstart[g], CD - begin)
            inner = inner_of(slot)
            k = (lanes + (128 - inner)) & 127
            keep = (k >= from_lane) & (k < to_lane)
            near = (LEAD + begin) // 128
            right = pltpu.roll(single_win[g], inner, axis=1)[:RUN_O]
            for i in range(ROWS_I):
                rows = pl.ds(i * NO + ostart[irr_i[i] ^ sym], RUN_O)
                value = turn(amps[near, rows, :], amps[near + 1, rows, :], LEAD + begin, inner, lanes)
                product = left[slot, pl.ds(i, 1), :] * right
                turned[i].append(jnp.where(keep, value + product, 0.0))
        for i in range(ROWS_I):
            for t, tile in enumerate(tiles_of(turned[i], lanes)):
                if t == 7:
                    tile = jnp.where(lanes < HALF, tile, 0.0)
                group[pl.ds(i * RUN_O, RUN_O), pl.ds(t * 128, 128)] = tile
        tau = group[...]
        top = tau.astype(jnp.bfloat16)
        out = pl.ds(pl.multiple_of(sym * GROUP, GROUP), GROUP)
        high[out, :] = top
        low[out, :] = (tau - top.astype(jnp.float32)).astype(jnp.bfloat16)
        return carry

    lax.fori_loop(0, IRREPS, symmetry, 0)


def spread_index(o, u, vir_ref, occ_ref, owner_ref, vlow, olow):
    block = jnp.int32(0)
    for k in range(64):
        block += jnp.where(owner_ref[k] == u, k, 0)
    lanes = lax.broadcasted_iota(jnp.int32, (8, 256), 1)
    row = lax.broadcasted_iota(jnp.int32, (8, 256), 0)
    column = jnp.where(row >= 4, SPAN - 4, 0) + block * 4 + row
    second = column >= NV
    sym = irrep_of(jnp.where(second, column - NV, column), vlow)
    sym = sym ^ jnp.where(second, vir_ref[1], vir_ref[0])
    i = jnp.zeros_like(lanes)
    irr_i = jnp.zeros_like(lanes)
    for n in range(ROWS_I):
        i = jnp.where(lanes >= n * NO, n, i)
        irr_i = jnp.where(lanes >= n * NO, occ_ref[o * ROWS_I + n], irr_i)
    j = lanes - i * NO
    irr_j = irrep_of(j, olow)
    begin = jnp.zeros_like(lanes)
    for g in range(1, IRREPS):
        begin = jnp.where(irr_j == g, olow[g], begin)
    lane = i * RUN_O + j - begin + jnp.where(row >= 4, HALF, 0)
    return jnp.where((sym ^ irr_i ^ irr_j) == 0, lane, -1)


def ladder_kernel(
    where_am_i,
    vir_ref,
    occ_ref,
    owner_ref,
    packed_ref,
    amp_ref,
    singles_ref,
    out_ref,
    index_ref,
    vstart,
    ostart,
    amps,
    ones,
    single_win,
    left,
    group,
    high,
    low,
    top,
    bottom,
):
    o, v = where_am_i()
    vlow = fill_starts(vir_ref, NV, vstart)
    olow = fill_starts(occ_ref, NO, ostart)
    pack_tau(o, v, vir_ref, occ_ref, vstart, ostart, amp_ref, singles_ref, amps, ones, single_win, left, group, high, low)
    index_ref[...] = spread_index(o, v, vir_ref, occ_ref, owner_ref, vlow, olow)
    for source in range(8):
        for s in range(2):
            wide = packed_ref[source, :, pl.ds(s * (FULL + 128), FULL)]
            last = packed_ref[source, :, pl.ds(FULL, 128)]
            if s == 1:
                last = pltpu.roll(last, HALF, axis=1)
            rows = pl.ds(s * SPAN + source * COLS, COLS)
            for part, at, size in ((wide, 0, FULL), (last, FULL, 128)):
                upper = part.astype(jnp.bfloat16)
                top[rows, pl.ds(at, size)] = upper
                bottom[rows, pl.ds(at, size)] = (part - upper.astype(jnp.float32)).astype(jnp.bfloat16)
    contract = functools.partial(
        lax.dot_general,
        dimension_numbers=(((1,), (1,)), ((), ())),
        preferred_element_type=jnp.float32,
    )
    upper, lower = top[...], bottom[...]
    sums = contract(upper, high[...]) + contract(lower, high[...]) + contract(upper, low[...])
    column = lax.broadcasted_iota(jnp.int32, (2 * SPAN, 128), 0)
    second = column >= NV
    sym = irrep_of(jnp.where(second, column - NV, column), vlow)
    sym = sym ^ jnp.where(second, vir_ref[1], vir_ref[0])
    pair = sym >> 1
    picked = sums[:, 0:128]
    for t in range(1, 4):
        picked = jnp.where(pair == t, sums[:, t * 128 : (t + 1) * 128], picked)
    span = (column >= SPAN).astype(jnp.int32)
    picked = jnp.where((sym & 1) == span, picked, pltpu.roll(picked, HALF, axis=1))
    lanes = lax.broadcasted_iota(jnp.int32, (SPAN, 128), 1)
    both = 0.5 * jnp.where(lanes < HALF, picked[:SPAN], picked[SPAN:])
    for k in range(64):
        out_ref[owner_ref[k]] = both[4 * k : 4 * k + 4, :]


def ladder(where_am_i, packed, amplitudes, singles, occ_irrep, vir_irrep, owner):
    smem = pl.BlockSpec(memory_space=pltpu.SMEM)
    vmem = pl.BlockSpec(memory_space=pltpu.VMEM)
    depth = SLOTS * 128
    return pl.pallas_call(
        functools.partial(ladder_kernel, where_am_i),
        in_specs=[smem, smem, smem, vmem, vmem, vmem],
        out_specs=[vmem, vmem],
        out_shape=[
            jax.ShapeDtypeStruct((64, 4, 128), jnp.float32),
            jax.ShapeDtypeStruct((8, 256), jnp.int32),
        ],
        scratch_shapes=[
            pltpu.SMEM((IRREPS + 1,), jnp.int32),
            pltpu.SMEM((IRREPS + 1,), jnp.int32),
            pltpu.VMEM((WIDE // 128, ROWS_I * NO + 16, 128), jnp.float32),
            pltpu.VMEM((5, NO + 16, 128), jnp.float32),
            pltpu.VMEM((IRREPS, 16, 128), jnp.float32),
            pltpu.VMEM((SLOTS, 8, 128), jnp.float32),
            pltpu.VMEM((GROUP, depth), jnp.float32),
            pltpu.VMEM((IRREPS * GROUP, depth), jnp.bfloat16),
            pltpu.VMEM((IRREPS * GROUP, depth), jnp.bfloat16),
            pltpu.VMEM((2 * SPAN, depth), jnp.bfloat16),
            pltpu.VMEM((2 * SPAN, depth), jnp.bfloat16),
        ],
        compiler_params=pltpu.CompilerParams(vmem_limit_bytes=HALF_VMEM),
        name="ladder",
    )(vir_irrep, occ_irrep, owner, packed, amplitudes, singles)


def finish_kernel(parts_ref, index_ref, out_ref):
    total = jnp.sum(parts_ref[...], axis=0)
    both = jnp.concatenate([total, total], axis=0)
    index = index_ref[...]
    lane = jnp.maximum(index, 0)
    near = jnp.take_along_axis(both, lane[:, :128], axis=1)
    far = jnp.take_along_axis(both, lane[:, 128:], axis=1)
    result = jnp.where(index >= 0, jnp.concatenate([near, far], axis=1), 0.0)
    out_ref[...] = result[:, : ROWS_I * NO]


def finish(parts, index):
    vmem = pl.BlockSpec(memory_space=pltpu.VMEM)
    return pl.pallas_call(
        finish_kernel,
        in_specs=[vmem, vmem],
        out_specs=vmem,
        out_shape=jax.ShapeDtypeStruct((8, ROWS_I * NO), jnp.float32),
        name="finish",
    )(parts, index)


def shards(amplitudes, singles, integrals, occ_irrep, vir_irrep, owner):
    packed = pack(placed, jnp.transpose(integrals, (0, 2, 1)), vir_irrep)
    gathered = lax.all_to_all(packed, "occ", 0, 0, tiled=True)
    mine, index = ladder(placed, gathered, amplitudes, singles, occ_irrep, vir_irrep, owner)
    parts = lax.all_to_all(mine, "vir", 0, 0, tiled=True)
    return jnp.transpose(finish(parts, index))


def solution(mesh):
    specs = (P("occ", "vir"), P(), P(None, "vir", "occ"), P(), P(), P())
    return jax.shard_map(
        shards, mesh=mesh, in_specs=specs, out_specs=P("occ", "vir"), check_vma=False
    )
```

```python
import functools

import jax
import jax.numpy as jnp
from jax import lax
from jax.experimental import pallas as pl
from jax.experimental.pallas import tpu as pltpu
from jax.sharding import PartitionSpec as P

NO = 40
NV = 480
SPAN = 256
IRREPS = 8
RUN_V = 120
RUN_O = 10
ROWS_I = 5
COLS = 32
CD = 3600
SLOTS = 8
LEAD = 256
WIDE = 33 * 128
MAIN = 28 * 128
GROUP = 64
PACK = 2 * SLOTS * RUN_V
ALL_VMEM = 64 * 1024 * 1024
SOME_VMEM = 12 * 1024 * 1024
FULL = 7 * 128
HALF = 64


def placed():
    return lax.axis_index("occ"), lax.axis_index("vir")


def fill_starts(labels, length, starts):
    bit = 1
    while bit * 2 <= length:
        bit *= 2
    low = [jnp.int32(0)] * IRREPS
    while bit:
        for g in range(1, IRREPS):
            cand = low[g] + bit
            below = labels[jnp.minimum(cand, length) - 1] < g
            low[g] = jnp.where((cand <= length) & below, cand, low[g])
        bit //= 2
    for g in range(IRREPS):
        starts[g] = low[g]
    starts[IRREPS] = jnp.int32(length)
    return low


def irrep_of(index, low):
    total = jnp.zeros_like(index)
    for g in range(1, IRREPS):
        total += (index >= low[g]).astype(jnp.int32)
    return total


def turn(near, far, position, inner, lanes):
    shift = lax.rem(position, 128)
    amount = lax.rem(inner + 128 - shift, 128)
    return pltpu.roll(jnp.where(lanes >= shift, near, far), amount, axis=1)


def inner_of(slot):
    return slot * RUN_V % 128


def tiles_of(turned, lanes):
    for slot in range(SLOTS - 1):
        yield jnp.where(lanes < inner_of(slot + 1), turned[slot], turned[slot + 1])
    yield turned[SLOTS - 1]


def first_pair(v):
    return (v * 15) // 2, (v % 2) * (NV // 2)


def pack_kernel(where_am_i, vir_hbm, int_hbm, out_hbm, labels, starts, ints, whole, packed, sems):
    label_copy = pltpu.make_async_copy(vir_hbm, labels, sems.at[0])
    label_copy.start()
    copies = []
    for s in range(2):
        copies.append(
            [
                pltpu.make_async_copy(
                    int_hbm.at[s, :, pl.ds(0, MAIN)],
                    ints.at[s, :, pl.ds(LEAD, MAIN)],
                    sems.at[1 + 2 * s],
                ),
                pltpu.make_async_copy(int_hbm.at[s], whole.at[s], sems.at[2 + 2 * s]),
            ]
        )
        for copy in copies[s]:
            copy.start()
    o, v = where_am_i()
    c_first, offset = first_pair(v)
    rest = WIDE - LEAD - MAIN - 128
    ints[:, :, pl.ds(0, LEAD)] = jnp.zeros((2, COLS, LEAD), jnp.float32)
    ints[:, :, pl.ds(LEAD + MAIN, 128)] = jnp.zeros((2, COLS, 128), jnp.float32)
    ints[:, :, pl.ds(LEAD + MAIN + 128, rest)] = jnp.zeros((2, COLS, rest), jnp.float32)
    label_copy.wait()
    low = fill_starts(labels, NV, starts)

    lanes = lax.broadcasted_iota(jnp.int32, (COLS, 128), 1)
    row = lax.broadcasted_iota(jnp.int32, (COLS, 128), 0)
    sends = []

    def send(at, size):
        for n in range(8):
            copy = pltpu.make_async_copy(
                packed.at[:, pl.ds(at, size)],
                out_hbm.at[n, :, pl.ds(at, size)],
                sems.at[5 + len(sends)],
            )
            copy.start()
            sends.append(copy)

    held = None
    for s in range(2):
        for copy in copies[s]:
            copy.wait()
        ints[s, :, pl.ds(LEAD + MAIN, CD - MAIN)] = whole[s, :, pl.ds(MAIN, CD - MAIN)]
        first = s * SPAN + o * COLS
        a = (first >= NV).astype(jnp.int32)
        b = first - a * NV
        irr_a = labels[a]
        irr_b = irrep_of(row + b, low)
        turned = []
        for slot in range(SLOTS):
            cross = labels[c_first + slot] ^ irr_a
            value = jnp.zeros((COLS, 128), jnp.float32)
            for h in range(IRREPS):
                position = LEAD + slot * NV + starts[cross ^ h] - offset
                base = pl.multiple_of((position // 128) * 128, 128)
                near = ints[s, :, pl.ds(base, 128)]
                far = ints[s, :, pl.ds(base + 128, 128)]
                moved = turn(near, far, position, inner_of(slot), lanes)
                value = jnp.where(irr_b == h, moved, value)
            turned.append(value)
            at = s * (FULL + 128)
            if slot:
                tile = jnp.where(lanes < inner_of(slot), turned[slot - 1], value)
                packed[:, pl.ds(at + (slot - 1) * 128, 128)] = tile
            if s == 1 and slot == 4:
                send(FULL + 128, 4 * 128)
        if s == 0:
            held = turned[7]
            send(0, FULL)
        else:
            packed[:, pl.ds(FULL, 128)] = jnp.where(
                lanes < HALF, held, pltpu.roll(turned[7], HALF, axis=1)
            )
            send(FULL, 128)
            send(FULL + 5 * 128, 3 * 128)
    for copy in sends:
        copy.wait()


def pack(where_am_i, integrals_t, vir_irrep):
    anywhere = pl.BlockSpec(memory_space=pl.ANY)
    return pl.pallas_call(
        functools.partial(pack_kernel, where_am_i),
        in_specs=[anywhere, anywhere],
        out_specs=anywhere,
        out_shape=jax.ShapeDtypeStruct((8, COLS, PACK), jnp.float32),
        scratch_shapes=[
            pltpu.SMEM((NV,), jnp.int32),
            pltpu.SMEM((IRREPS + 1,), jnp.int32),
            pltpu.VMEM((2, COLS, WIDE), jnp.float32),
            pltpu.VMEM((2, COLS, CD), jnp.float32),
            pltpu.VMEM((COLS, PACK), jnp.float32),
            pltpu.SemaphoreType.DMA((5 + 32,)),
        ],
        compiler_params=pltpu.CompilerParams(vmem_limit_bytes=ALL_VMEM),
        name="pack",
    )(vir_irrep, integrals_t)


def pack_tau(o, v, vir_ref, occ_ref, vstart, ostart, amp_ref, singles_ref, amps, ones, single_win, left, group, high, low):
    c_first, offset = first_pair(v)
    for t in range(CD // 128 + 1):
        size = min(128, CD - t * 128)
        amps[LEAD // 128 + t, pl.ds(0, ROWS_I * NO), pl.ds(0, size)] = amp_ref[:, pl.ds(t * 128, size)]
    amps[:, pl.ds(ROWS_I * NO, 16), :] = jnp.zeros((WIDE // 128, 16, 128), jnp.float32)

    ones[...] = jnp.zeros_like(ones)
    for t in range(4):
        size = min(128, NV - t * 128)
        ones[t, pl.ds(0, NO), pl.ds(0, size)] = singles_ref[:, pl.ds(t * 128, size)]
    lanes_w = lax.broadcasted_iota(jnp.int32, (16, 128), 1)
    for g in range(IRREPS):
        at, rows = vstart[g], pl.ds(ostart[g], 16)
        single_win[g] = turn(ones[at // 128, rows, :], ones[at // 128 + 1, rows, :], at, 0, lanes_w)
    lane_c = lax.broadcasted_iota(jnp.int32, (8, 128), 1)
    row_i = lax.broadcasted_iota(jnp.int32, (8, 1), 0)
    irr_i = [occ_ref[o * ROWS_I + i] for i in range(ROWS_I)]
    for slot in range(SLOTS):
        c = c_first + slot
        irr_c = vir_ref[c]
        own = ones[c // 128, pl.ds(o * ROWS_I, 8), :]
        column = jnp.sum(jnp.where(lane_c == lax.rem(c, 128), own, 0.0), axis=1, keepdims=True)
        for i in range(ROWS_I):
            column = jnp.where((row_i == i) & (irr_i[i] != irr_c), 0.0, column)
        left[slot] = jnp.broadcast_to(column, (8, 128))

    lanes = lax.broadcasted_iota(jnp.int32, (RUN_O, 128), 1)
    group[...] = jnp.zeros_like(group)

    def symmetry(sym, carry):
        turned = [[] for _ in range(ROWS_I)]
        for slot in range(SLOTS):
            g = vir_ref[c_first + slot] ^ sym
            begin = slot * NV + vstart[g] - offset
            from_lane = jnp.maximum(0, -begin)
            to_lane = jnp.minimum(vstart[g + 1] - vstart[g], CD - begin)
            inner = inner_of(slot)
            k = (lanes + (128 - inner)) & 127
            keep = (k >= from_lane) & (k < to_lane)
            near = (LEAD + begin) // 128
            right = pltpu.roll(single_win[g], inner, axis=1)[:RUN_O]
            for i in range(ROWS_I):
                rows = pl.ds(i * NO + ostart[irr_i[i] ^ sym], RUN_O)
                value = turn(amps[near, rows, :], amps[near + 1, rows, :], LEAD + begin, inner, lanes)
                product = left[slot, pl.ds(i, 1), :] * right
                turned[i].append(jnp.where(keep, value + product, 0.0))
        for i in range(ROWS_I):
            for t, tile in enumerate(tiles_of(turned[i], lanes)):
                if t == 7:
                    tile = jnp.where(lanes < HALF, tile, 0.0)
                group[pl.ds(i * RUN_O, RUN_O), pl.ds(t * 128, 128)] = tile
        tau = group[...]
        top = tau.astype(jnp.bfloat16)
        out = pl.ds(pl.multiple_of(sym * GROUP, GROUP), GROUP)
        high[out, :] = top
        low[out, :] = (tau - top.astype(jnp.float32)).astype(jnp.bfloat16)
        return carry

    lax.fori_loop(0, IRREPS, symmetry, 0)


def spread_index(o, u, vir_ref, occ_ref, owner_ref, vlow, olow):
    block = jnp.int32(0)
    for k in range(64):
        block += jnp.where(owner_ref[k] == u, k, 0)
    lanes = lax.broadcasted_iota(jnp.int32, (8, 256), 1)
    row = lax.broadcasted_iota(jnp.int32, (8, 256), 0)
    column = jnp.where(row >= 4, SPAN - 4, 0) + block * 4 + row
    second = column >= NV
    sym = irrep_of(jnp.where(second, column - NV, column), vlow)
    sym = sym ^ jnp.where(second, vir_ref[1], vir_ref[0])
    i = jnp.zeros_like(lanes)
    irr_i = jnp.zeros_like(lanes)
    for n in range(ROWS_I):
        i = jnp.where(lanes >= n * NO, n, i)
        irr_i = jnp.where(lanes >= n * NO, occ_ref[o * ROWS_I + n], irr_i)
    j = lanes - i * NO
    irr_j = irrep_of(j, olow)
    begin = jnp.zeros_like(lanes)
    for g in range(1, IRREPS):
        begin = jnp.where(irr_j == g, olow[g], begin)
    lane = i * RUN_O + j - begin + jnp.where(row >= 4, HALF, 0)
    return jnp.where((sym ^ irr_i ^ irr_j) == 0, lane, -1)


def tau_kernel(
    where_am_i,
    vir_ref,
    occ_ref,
    owner_ref,
    amp_ref,
    singles_ref,
    high,
    low,
    index_ref,
    vstart,
    ostart,
    amps,
    ones,
    single_win,
    left,
    group,
):
    o, v = where_am_i()
    vlow = fill_starts(vir_ref, NV, vstart)
    olow = fill_starts(occ_ref, NO, ostart)
    pack_tau(o, v, vir_ref, occ_ref, vstart, ostart, amp_ref, singles_ref, amps, ones, single_win, left, group, high, low)
    index_ref[...] = spread_index(o, v, vir_ref, occ_ref, owner_ref, vlow, olow)


def tau(where_am_i, amplitudes, singles, occ_irrep, vir_irrep, owner):
    smem = pl.BlockSpec(memory_space=pltpu.SMEM)
    vmem = pl.BlockSpec(memory_space=pltpu.VMEM)
    depth = SLOTS * 128
    return pl.pallas_call(
        functools.partial(tau_kernel, where_am_i),
        in_specs=[smem, smem, smem, vmem, vmem],
        out_specs=[vmem, vmem, vmem],
        out_shape=[
            jax.ShapeDtypeStruct((IRREPS * GROUP, depth), jnp.bfloat16),
            jax.ShapeDtypeStruct((IRREPS * GROUP, depth), jnp.bfloat16),
            jax.ShapeDtypeStruct((8, 256), jnp.int32),
        ],
        scratch_shapes=[
            pltpu.SMEM((IRREPS + 1,), jnp.int32),
            pltpu.SMEM((IRREPS + 1,), jnp.int32),
            pltpu.VMEM((WIDE // 128, ROWS_I * NO + 16, 128), jnp.float32),
            pltpu.VMEM((5, NO + 16, 128), jnp.float32),
            pltpu.VMEM((IRREPS, 16, 128), jnp.float32),
            pltpu.VMEM((SLOTS, 8, 128), jnp.float32),
            pltpu.VMEM((GROUP, depth), jnp.float32),
        ],
        compiler_params=pltpu.CompilerParams(vmem_limit_bytes=SOME_VMEM),
        cost_estimate=pl.CostEstimate(flops=0, bytes_accessed=8 * 1024 * 1024, transcendentals=0),
        name="tau",
    )(vir_irrep, occ_irrep, owner, amplitudes, singles)


def ladder_kernel(vir_ref, owner_ref, packed_ref, high, low, out_ref, vstart, top, bottom):
    vlow = fill_starts(vir_ref, NV, vstart)
    for source in range(8):
        for s in range(2):
            wide = packed_ref[source, :, pl.ds(s * (FULL + 128), FULL)]
            last = packed_ref[source, :, pl.ds(FULL, 128)]
            if s == 1:
                last = pltpu.roll(last, HALF, axis=1)
            rows = pl.ds(s * SPAN + source * COLS, COLS)
            for part, at, size in ((wide, 0, FULL), (last, FULL, 128)):
                upper = part.astype(jnp.bfloat16)
                top[rows, pl.ds(at, size)] = upper
                bottom[rows, pl.ds(at, size)] = (part - upper.astype(jnp.float32)).astype(jnp.bfloat16)
    contract = functools.partial(
        lax.dot_general,
        dimension_numbers=(((1,), (1,)), ((), ())),
        preferred_element_type=jnp.float32,
    )
    upper, lower = top[...], bottom[...]
    sums = contract(upper, high[...]) + contract(lower, high[...]) + contract(upper, low[...])
    column = lax.broadcasted_iota(jnp.int32, (2 * SPAN, 128), 0)
    second = column >= NV
    sym = irrep_of(jnp.where(second, column - NV, column), vlow)
    sym = sym ^ jnp.where(second, vir_ref[1], vir_ref[0])
    pair = sym >> 1
    picked = sums[:, 0:128]
    for t in range(1, 4):
        picked = jnp.where(pair == t, sums[:, t * 128 : (t + 1) * 128], picked)
    span = (column >= SPAN).astype(jnp.int32)
    picked = jnp.where((sym & 1) == span, picked, pltpu.roll(picked, HALF, axis=1))
    lanes = lax.broadcasted_iota(jnp.int32, (SPAN, 128), 1)
    both = 0.5 * jnp.where(lanes < HALF, picked[:SPAN], picked[SPAN:])
    for k in range(64):
        out_ref[owner_ref[k]] = both[4 * k : 4 * k + 4, :]


def ladder(packed, high, low, vir_irrep, owner):
    smem = pl.BlockSpec(memory_space=pltpu.SMEM)
    vmem = pl.BlockSpec(memory_space=pltpu.VMEM)
    depth = SLOTS * 128
    return pl.pallas_call(
        ladder_kernel,
        in_specs=[smem, smem, vmem, vmem, vmem],
        out_specs=vmem,
        out_shape=jax.ShapeDtypeStruct((64, 4, 128), jnp.float32),
        scratch_shapes=[
            pltpu.SMEM((IRREPS + 1,), jnp.int32),
            pltpu.VMEM((2 * SPAN, depth), jnp.bfloat16),
            pltpu.VMEM((2 * SPAN, depth), jnp.bfloat16),
        ],
        compiler_params=pltpu.CompilerParams(vmem_limit_bytes=SOME_VMEM),
        name="ladder",
    )(vir_irrep, owner, packed, high, low)


def finish_kernel(parts_ref, index_ref, out_ref):
    total = jnp.sum(parts_ref[...], axis=0)
    both = jnp.concatenate([total, total], axis=0)
    index = index_ref[...]
    lane = jnp.maximum(index, 0)
    near = jnp.take_along_axis(both, lane[:, :128], axis=1)
    far = jnp.take_along_axis(both, lane[:, 128:], axis=1)
    result = jnp.where(index >= 0, jnp.concatenate([near, far], axis=1), 0.0)
    out_ref[...] = result[:, : ROWS_I * NO]


def finish(parts, index):
    vmem = pl.BlockSpec(memory_space=pltpu.VMEM)
    return pl.pallas_call(
        finish_kernel,
        in_specs=[vmem, vmem],
        out_specs=vmem,
        out_shape=jax.ShapeDtypeStruct((8, ROWS_I * NO), jnp.float32),
        compiler_params=pltpu.CompilerParams(vmem_limit_bytes=1024 * 1024),
        name="finish",
    )(parts, index)


def shards(amplitudes, singles, integrals, occ_irrep, vir_irrep, owner):
    packed = pack(placed, jnp.transpose(integrals, (0, 2, 1)), vir_irrep)
    gathered = lax.all_to_all(packed, "occ", 0, 0, tiled=True)
    high, low, index = tau(placed, amplitudes, singles, occ_irrep, vir_irrep, owner)
    mine = ladder(gathered, high, low, vir_irrep, owner)
    parts = lax.all_to_all(mine, "vir", 0, 0, tiled=True)
    return jnp.transpose(finish(parts, index))


def solution(mesh):
    specs = (P("occ", "vir"), P(), P(None, "vir", "occ"), P(), P(), P())
    return jax.shard_map(
        shards, mesh=mesh, in_specs=specs, out_specs=P("occ", "vir"), check_vma=False
    )
```

```python
import functools

import jax
import jax.numpy as jnp
from jax import lax
from jax.experimental import pallas as pl
from jax.experimental.pallas import tpu as pltpu
from jax.sharding import PartitionSpec as P

NO = 40
NV = 480
SPAN = 256
IRREPS = 8
RUN_V = 120
RUN_O = 10
ROWS_I = 5
COLS = 32
CD = 3600
SLOTS = 8
LEAD = 256
WIDE = 33 * 128
MAIN = 28 * 128
GROUP = 50
PACK = 2 * SLOTS * RUN_V
ALL_VMEM = 64 * 1024 * 1024
SOME_VMEM = 12 * 1024 * 1024
FULL = 7 * 128
HALF = 64


def placed():
    return lax.axis_index("occ"), lax.axis_index("vir")


def fill_starts(labels, length, starts):
    bit = 1
    while bit * 2 <= length:
        bit *= 2
    low = [jnp.int32(0)] * IRREPS
    while bit:
        for g in range(1, IRREPS):
            cand = low[g] + bit
            below = labels[jnp.minimum(cand, length) - 1] < g
            low[g] = jnp.where(below, cand, low[g])
        bit //= 2
    for g in range(IRREPS):
        starts[g] = low[g]
    starts[IRREPS] = jnp.int32(length)
    return low


def irrep_of(index, low):
    total = jnp.zeros_like(index)
    for g in range(1, IRREPS):
        total += (index >= low[g]).astype(jnp.int32)
    return total


def turn(near, far, position, inner, lanes):
    shift = lax.rem(position, 128)
    amount = lax.rem(inner + 128 - shift, 128)
    return pltpu.roll(jnp.where(lanes >= shift, near, far), amount, axis=1)


def inner_of(slot):
    return slot * RUN_V % 128


def tiles_of(turned, lanes):
    for slot in range(SLOTS - 1):
        yield jnp.where(lanes < inner_of(slot + 1), turned[slot], turned[slot + 1])
    yield turned[SLOTS - 1]


def first_pair(v):
    return (v * 15) // 2, (v % 2) * (NV // 2)


def pack_kernel(where_am_i, vir_hbm, int_hbm, out_hbm, labels, starts, ints, whole, packed, sems):
    label_copy = pltpu.make_async_copy(vir_hbm, labels, sems.at[0])
    label_copy.start()
    copies = []
    for s in range(2):
        copies.append(
            [
                pltpu.make_async_copy(
                    int_hbm.at[s, :, pl.ds(0, MAIN)],
                    ints.at[s, :, pl.ds(LEAD, MAIN)],
                    sems.at[1 + 2 * s],
                ),
                pltpu.make_async_copy(int_hbm.at[s], whole.at[s], sems.at[2 + 2 * s]),
            ]
        )
        for copy in copies[s]:
            copy.start()
    o, v = where_am_i()
    c_first, offset = first_pair(v)
    rest = WIDE - LEAD - MAIN - 128
    ints[:, :, pl.ds(0, LEAD)] = jnp.zeros((2, COLS, LEAD), jnp.float32)
    ints[:, :, pl.ds(LEAD + MAIN, 128)] = jnp.zeros((2, COLS, 128), jnp.float32)
    ints[:, :, pl.ds(LEAD + MAIN + 128, rest)] = jnp.zeros((2, COLS, rest), jnp.float32)
    label_copy.wait()
    low = fill_starts(labels, NV, starts)

    lanes = lax.broadcasted_iota(jnp.int32, (COLS, 128), 1)
    row = lax.broadcasted_iota(jnp.int32, (COLS, 128), 0)
    sends = []

    def send(at, size):
        for n in range(8):
            copy = pltpu.make_async_copy(
                packed.at[:, pl.ds(at, size)],
                out_hbm.at[n, :, pl.ds(at, size)],
                sems.at[5 + len(sends)],
            )
            copy.start()
            sends.append(copy)

    held = None
    for s in range(2):
        for copy in copies[s]:
            copy.wait()
        ints[s, :, pl.ds(LEAD + MAIN, CD - MAIN)] = whole[s, :, pl.ds(MAIN, CD - MAIN)]
        first = s * SPAN + o * COLS
        a = (first >= NV).astype(jnp.int32)
        b = first - a * NV
        irr_a = labels[a]
        irr_b = irrep_of(row + b, low)
        turned = []
        for slot in range(SLOTS):
            cross = labels[c_first + slot] ^ irr_a
            value = jnp.zeros((COLS, 128), jnp.float32)
            for h in range(IRREPS):
                position = LEAD + slot * NV + starts[cross ^ h] - offset
                base = pl.multiple_of((position // 128) * 128, 128)
                near = ints[s, :, pl.ds(base, 128)]
                far = ints[s, :, pl.ds(base + 128, 128)]
                moved = turn(near, far, position, inner_of(slot), lanes)
                value = jnp.where(irr_b == h, moved, value)
            turned.append(value)
            at = s * (FULL + 128)
            if slot:
                tile = jnp.where(lanes < inner_of(slot), turned[slot - 1], value)
                packed[:, pl.ds(at + (slot - 1) * 128, 128)] = tile
            if s == 1 and slot == 4:
                send(FULL + 128, 4 * 128)
        if s == 0:
            held = turned[7]
            send(0, FULL)
        else:
            packed[:, pl.ds(FULL, 128)] = jnp.where(
                lanes < HALF, held, pltpu.roll(turned[7], HALF, axis=1)
            )
            send(FULL, 128)
            send(FULL + 5 * 128, 3 * 128)
    for copy in sends:
        copy.wait()


def pack(where_am_i, integrals_t, vir_irrep):
    anywhere = pl.BlockSpec(memory_space=pl.ANY)
    return pl.pallas_call(
        functools.partial(pack_kernel, where_am_i),
        in_specs=[anywhere, anywhere],
        out_specs=anywhere,
        out_shape=jax.ShapeDtypeStruct((8, COLS, PACK), jnp.float32),
        scratch_shapes=[
            pltpu.SMEM((NV,), jnp.int32),
            pltpu.SMEM((IRREPS + 1,), jnp.int32),
            pltpu.VMEM((2, COLS, WIDE), jnp.float32),
            pltpu.VMEM((2, COLS, CD), jnp.float32),
            pltpu.VMEM((COLS, PACK), jnp.float32),
            pltpu.SemaphoreType.DMA((5 + 32,)),
        ],
        compiler_params=pltpu.CompilerParams(vmem_limit_bytes=ALL_VMEM),
        name="pack",
    )(vir_irrep, integrals_t)


def pack_tau(o, v, vir_ref, occ_ref, vstart, ostart, amp_ref, singles_ref, amps, ones, single_win, left, group, high, low):
    c_first, offset = first_pair(v)
    for t in range(CD // 128 + 1):
        size = min(128, CD - t * 128)
        amps[LEAD // 128 + t, pl.ds(0, ROWS_I * NO), pl.ds(0, size)] = amp_ref[:, pl.ds(t * 128, size)]
    amps[:, pl.ds(ROWS_I * NO, 16), :] = jnp.zeros((WIDE // 128, 16, 128), jnp.float32)

    ones[...] = jnp.zeros_like(ones)
    for t in range(4):
        size = min(128, NV - t * 128)
        ones[t, pl.ds(0, NO), pl.ds(0, size)] = singles_ref[:, pl.ds(t * 128, size)]
    lanes_w = lax.broadcasted_iota(jnp.int32, (16, 128), 1)
    for g in range(IRREPS):
        at, rows = vstart[g], pl.ds(ostart[g], 16)
        single_win[g] = turn(ones[at // 128, rows, :], ones[at // 128 + 1, rows, :], at, 0, lanes_w)
    lane_c = lax.broadcasted_iota(jnp.int32, (8, 128), 1)
    row_i = lax.broadcasted_iota(jnp.int32, (8, 1), 0)
    irr_i = [occ_ref[o * ROWS_I + i] for i in range(ROWS_I)]
    for slot in range(SLOTS):
        c = c_first + slot
        irr_c = vir_ref[c]
        own = ones[c // 128, pl.ds(o * ROWS_I, 8), :]
        column = jnp.sum(jnp.where(lane_c == lax.rem(c, 128), own, 0.0), axis=1, keepdims=True)
        for i in range(ROWS_I):
            column = jnp.where((row_i == i) & (irr_i[i] != irr_c), 0.0, column)
        left[slot] = jnp.broadcast_to(column, (8, 128))

    lanes = lax.broadcasted_iota(jnp.int32, (RUN_O, 128), 1)
    for sym in range(IRREPS):
        turned = [[] for _ in range(ROWS_I)]
        for slot in range(SLOTS):
            g = vir_ref[c_first + slot] ^ sym
            begin = slot * NV + vstart[g] - offset
            from_lane = jnp.maximum(0, -begin)
            to_lane = jnp.minimum(vstart[g + 1] - vstart[g], CD - begin)
            inner = inner_of(slot)
            k = (lanes + (128 - inner)) & 127
            keep = (k >= from_lane) & (k < to_lane)
            near = (LEAD + begin) // 128
            right = pltpu.roll(single_win[g], inner, axis=1)[:RUN_O]
            for i in range(ROWS_I):
                rows = pl.ds(i * NO + ostart[irr_i[i] ^ sym], RUN_O)
                value = turn(amps[near, rows, :], amps[near + 1, rows, :], LEAD + begin, inner, lanes)
                product = left[slot, pl.ds(i, 1), :] * right
                turned[i].append(jnp.where(keep, value + product, 0.0))
        for i in range(ROWS_I):
            for t, tile in enumerate(tiles_of(turned[i], lanes)):
                if t == 7:
                    tile = jnp.where(lanes < HALF, tile, 0.0)
                group[pl.ds(sym * GROUP + i * RUN_O, RUN_O), pl.ds(t * 128, 128)] = tile
    wide = group[:, pl.ds(0, FULL)]
    top = wide.astype(jnp.bfloat16)
    high[:, pl.ds(0, FULL)] = top
    low[...] = (wide - top.astype(jnp.float32)).astype(jnp.bfloat16)
    last = group[:, pl.ds(FULL, 128)]
    upper = last.astype(jnp.bfloat16).astype(jnp.float32)
    lanes_all = lax.broadcasted_iota(jnp.int32, last.shape, 1)
    last = jnp.where(lanes_all < HALF, upper, pltpu.roll(last - upper, HALF, axis=1))
    high[:, pl.ds(FULL, 128)] = last.astype(jnp.bfloat16)


def spread_index(o, u, vir_ref, occ_ref, owner_ref, vlow, olow):
    block = jnp.int32(0)
    for k in range(64):
        block += jnp.where(owner_ref[k] == u, k, 0)
    lanes = lax.broadcasted_iota(jnp.int32, (8, 256), 1)
    row = lax.broadcasted_iota(jnp.int32, (8, 256), 0)
    column = jnp.where(row >= 4, SPAN - 4, 0) + block * 4 + row
    second = column >= NV
    sym = irrep_of(jnp.where(second, column - NV, column), vlow)
    sym = sym ^ jnp.where(second, vir_ref[1], vir_ref[0])
    i = jnp.zeros_like(lanes)
    irr_i = jnp.zeros_like(lanes)
    for n in range(ROWS_I):
        i = jnp.where(lanes >= n * NO, n, i)
        irr_i = jnp.where(lanes >= n * NO, occ_ref[o * ROWS_I + n], irr_i)
    j = lanes - i * NO
    irr_j = irrep_of(j, olow)
    begin = jnp.zeros_like(lanes)
    for g in range(1, IRREPS):
        begin = jnp.where(irr_j == g, olow[g], begin)
    lane = i * RUN_O + j - begin + jnp.where(row >= 4, HALF, 0)
    return jnp.where((sym ^ irr_i ^ irr_j) == 0, lane, -1)


def tau_kernel(
    where_am_i,
    vir_ref,
    occ_ref,
    owner_ref,
    amp_ref,
    singles_ref,
    high,
    low,
    index_ref,
    vstart,
    ostart,
    amps,
    ones,
    single_win,
    left,
    group,
):
    o, v = where_am_i()
    vlow = fill_starts(vir_ref, NV, vstart)
    olow = fill_starts(occ_ref, NO, ostart)
    pack_tau(o, v, vir_ref, occ_ref, vstart, ostart, amp_ref, singles_ref, amps, ones, single_win, left, group, high, low)
    index_ref[...] = spread_index(o, v, vir_ref, occ_ref, owner_ref, vlow, olow)


def tau(where_am_i, amplitudes, singles, occ_irrep, vir_irrep, owner):
    smem = pl.BlockSpec(memory_space=pltpu.SMEM)
    vmem = pl.BlockSpec(memory_space=pltpu.VMEM)
    depth = SLOTS * 128
    return pl.pallas_call(
        functools.partial(tau_kernel, where_am_i),
        in_specs=[smem, smem, smem, vmem, vmem],
        out_specs=[vmem, vmem, vmem],
        out_shape=[
            jax.ShapeDtypeStruct((IRREPS * GROUP, depth), jnp.bfloat16),
            jax.ShapeDtypeStruct((IRREPS * GROUP, FULL), jnp.bfloat16),
            jax.ShapeDtypeStruct((8, 256), jnp.int32),
        ],
        scratch_shapes=[
            pltpu.SMEM((IRREPS + 1,), jnp.int32),
            pltpu.SMEM((IRREPS + 1,), jnp.int32),
            pltpu.VMEM((WIDE // 128, ROWS_I * NO + 16, 128), jnp.float32),
            pltpu.VMEM((5, NO + 16, 128), jnp.float32),
            pltpu.VMEM((IRREPS, 16, 128), jnp.float32),
            pltpu.VMEM((SLOTS, 8, 128), jnp.float32),
            pltpu.VMEM((IRREPS * GROUP, depth), jnp.float32),
        ],
        compiler_params=pltpu.CompilerParams(vmem_limit_bytes=SOME_VMEM),
        cost_estimate=pl.CostEstimate(flops=0, bytes_accessed=8 * 1024 * 1024, transcendentals=0),
        name="tau",
    )(vir_irrep, occ_irrep, owner, amplitudes, singles)


def ladder_kernel(vir_ref, owner_ref, packed_ref, high, low, out_ref, vstart, top, bottom, sums):
    vlow = fill_starts(vir_ref, NV, vstart)
    lanes = lax.broadcasted_iota(jnp.int32, (COLS, 128), 1)
    for source in range(8):
        last = packed_ref[source, :, pl.ds(FULL, 128)]
        other = pltpu.roll(last, HALF, axis=1)
        for s in range(2):
            rows = pl.ds(s * SPAN + source * COLS, COLS)
            wide = packed_ref[source, :, pl.ds(s * (FULL + 128), FULL)]
            upper = wide.astype(jnp.bfloat16)
            top[rows, pl.ds(0, FULL)] = upper
            bottom[rows, pl.ds(0, FULL)] = (wide - upper.astype(jnp.float32)).astype(jnp.bfloat16)
            twice = jnp.where(lanes < HALF, last, other) if s == 0 else jnp.where(lanes < HALF, other, last)
            upper = twice.astype(jnp.bfloat16)
            top[rows, pl.ds(FULL, 128)] = upper
            rest = jnp.where(lanes < HALF, twice - upper.astype(jnp.float32), 0.0)
            bottom[rows, pl.ds(FULL, 128)] = rest.astype(jnp.bfloat16)
    contract = functools.partial(
        lax.dot_general,
        dimension_numbers=(((1,), (1,)), ((), ())),
        preferred_element_type=jnp.float32,
    )
    used = IRREPS * GROUP
    sums[pl.ds(0, used), :] = (
        contract(high[...], top[...])
        + contract(high[...], bottom[...])
        + contract(low[...], top[:, pl.ds(0, FULL)])
    )
    sums[pl.ds(used, 8), :] = jnp.zeros((8, 2 * SPAN), jnp.float32)
    halves = []
    for s in range(2):
        there = pl.ds(s * SPAN, SPAN)
        column = lax.broadcasted_iota(jnp.int32, (56, SPAN), 1) + s * SPAN
        second = column >= NV
        sym = irrep_of(jnp.where(second, column - NV, column), vlow)
        sym = sym ^ jnp.where(second, vir_ref[1], vir_ref[0])
        picked = sums[pl.ds(0, 56), there]
        for g in range(1, IRREPS):
            picked = jnp.where(sym == g, sums[pl.ds(g * GROUP, 56), there], picked)
        halves += [picked, jnp.zeros((HALF - 56, SPAN), jnp.float32)]
    both = 0.5 * jnp.transpose(jnp.concatenate(halves, axis=0))
    for k in range(64):
        out_ref[owner_ref[k]] = both[4 * k : 4 * k + 4, :]


def ladder(packed, high, low, vir_irrep, owner):
    smem = pl.BlockSpec(memory_space=pltpu.SMEM)
    vmem = pl.BlockSpec(memory_space=pltpu.VMEM)
    depth = SLOTS * 128
    return pl.pallas_call(
        ladder_kernel,
        in_specs=[smem, smem, vmem, vmem, vmem],
        out_specs=vmem,
        out_shape=jax.ShapeDtypeStruct((64, 4, 128), jnp.float32),
        scratch_shapes=[
            pltpu.SMEM((IRREPS + 1,), jnp.int32),
            pltpu.VMEM((2 * SPAN, depth), jnp.bfloat16),
            pltpu.VMEM((2 * SPAN, depth), jnp.bfloat16),
            pltpu.VMEM((IRREPS * GROUP + 8, 2 * SPAN), jnp.float32),
        ],
        compiler_params=pltpu.CompilerParams(vmem_limit_bytes=SOME_VMEM),
        name="ladder",
    )(vir_irrep, owner, packed, high, low)


def finish_kernel(parts_ref, index_ref, out_ref):
    total = jnp.sum(parts_ref[...], axis=0)
    both = jnp.concatenate([total, total], axis=0)
    index = index_ref[...]
    lane = jnp.maximum(index, 0)
    near = jnp.take_along_axis(both, lane[:, :128], axis=1)
    far = jnp.take_along_axis(both, lane[:, 128:], axis=1)
    result = jnp.where(index >= 0, jnp.concatenate([near, far], axis=1), 0.0)
    out_ref[...] = result[:, : ROWS_I * NO]


def finish(parts, index):
    vmem = pl.BlockSpec(memory_space=pltpu.VMEM)
    return pl.pallas_call(
        finish_kernel,
        in_specs=[vmem, vmem],
        out_specs=vmem,
        out_shape=jax.ShapeDtypeStruct((8, ROWS_I * NO), jnp.float32),
        compiler_params=pltpu.CompilerParams(vmem_limit_bytes=1024 * 1024),
        name="finish",
    )(parts, index)


def shards(amplitudes, singles, integrals, occ_irrep, vir_irrep, owner):
    packed = pack(placed, jnp.transpose(integrals, (0, 2, 1)), vir_irrep)
    gathered = lax.all_to_all(packed, "occ", 0, 0, tiled=True)
    high, low, index = tau(placed, amplitudes, singles, occ_irrep, vir_irrep, owner)
    mine = ladder(gathered, high, low, vir_irrep, owner)
    parts = lax.all_to_all(mine, "vir", 0, 0, tiled=True)
    return jnp.transpose(finish(parts, index))


def solution(mesh):
    specs = (P("occ", "vir"), P(), P(None, "vir", "occ"), P(), P(), P())
    return jax.shard_map(
        shards, mesh=mesh, in_specs=specs, out_specs=P("occ", "vir"), check_vma=False
    )
```

```python
import functools

import jax
import jax.numpy as jnp
from jax import lax
from jax.experimental import pallas as pl
from jax.experimental.pallas import tpu as pltpu
from jax.sharding import PartitionSpec as P

NO = 40
NV = 480
SPAN = 256
IRREPS = 8
RUN_V = 120
RUN_O = 10
ROWS_I = 5
COLS = 32
CD = 3600
SLOTS = 8
LEAD = 256
WIDE = 33 * 128
MAIN = 28 * 128
GROUP = 50
PACK = 2 * SLOTS * RUN_V
ALL_VMEM = 64 * 1024 * 1024
SOME_VMEM = 12 * 1024 * 1024
FULL = 7 * 128
HALF = 64


def placed():
    return lax.axis_index("occ"), lax.axis_index("vir")


def fill_starts(labels, length, starts):
    bit = 1
    while bit * 2 <= length:
        bit *= 2
    low = [jnp.int32(0)] * IRREPS
    while bit:
        for g in range(1, IRREPS):
            cand = low[g] + bit
            below = labels[jnp.minimum(cand, length) - 1] < g
            low[g] = jnp.where(below, cand, low[g])
        bit //= 2
    for g in range(IRREPS):
        starts[g] = low[g]
    starts[IRREPS] = jnp.int32(length)
    return low


def irrep_of(index, low):
    total = jnp.zeros_like(index)
    for g in range(1, IRREPS):
        total += (index >= low[g]).astype(jnp.int32)
    return total


def turn(near, far, position, inner, lanes):
    shift = position & 127
    amount = (inner + 128 - shift) & 127
    return pltpu.roll(jnp.where(lanes >= shift, near, far), amount, axis=1)


def inner_of(slot):
    return slot * RUN_V % 128


def tiles_of(turned, lanes):
    for slot in range(SLOTS - 1):
        yield jnp.where(lanes < inner_of(slot + 1), turned[slot], turned[slot + 1])
    yield turned[SLOTS - 1]


def first_pair(v):
    return (v * 15) >> 1, (v & 1) * (NV // 2)


def pack_kernel(where_am_i, vir_hbm, int_hbm, out_hbm, labels, starts, ints, whole, packed, sems):
    label_copy = pltpu.make_async_copy(vir_hbm, labels, sems.at[0])
    label_copy.start()
    copies = []
    for s in range(2):
        copies.append(
            [
                pltpu.make_async_copy(int_hbm.at[s], whole.at[s], sems.at[2 + 2 * s]),
            ]
        )
        for copy in copies[s]:
            copy.start()
    o, v = where_am_i()
    c_first, offset = first_pair(v)
    rest = WIDE - LEAD - MAIN - 128
    ints[:, :, pl.ds(0, LEAD)] = jnp.zeros((2, COLS, LEAD), jnp.float32)
    ints[:, :, pl.ds(LEAD + MAIN, 128)] = jnp.zeros((2, COLS, 128), jnp.float32)
    ints[:, :, pl.ds(LEAD + MAIN + 128, rest)] = jnp.zeros((2, COLS, rest), jnp.float32)
    label_copy.wait()
    low = fill_starts(labels, NV, starts)

    lanes = lax.broadcasted_iota(jnp.int32, (COLS, 128), 1)
    row = lax.broadcasted_iota(jnp.int32, (COLS, 128), 0)
    sends = []

    def send(at, size):
        for n in range(8):
            copy = pltpu.make_async_copy(
                packed.at[:, pl.ds(at, size)],
                out_hbm.at[n, :, pl.ds(at, size)],
                sems.at[5 + len(sends)],
            )
            copy.start()
            sends.append(copy)

    held = None
    irr_c = [labels[c_first + slot] for slot in range(SLOTS)]
    begin = [LEAD - offset + low[g] for g in range(IRREPS)]
    for s in range(2):
        for copy in copies[s]:
            copy.wait()
        ints[s, :, pl.ds(LEAD, CD)] = whole[s]
        first = s * SPAN + o * COLS
        a = (first >= NV).astype(jnp.int32)
        b = first - a * NV
        irr_a = labels[a]
        irr_b = irrep_of(row + b, low)
        turned = []
        for slot in range(SLOTS):
            cross = irr_c[slot] ^ irr_a
            mine = irr_b ^ cross
            value = jnp.zeros((COLS, 128), jnp.float32)
            for g in range(IRREPS):
                position = begin[g] + slot * NV
                base = pl.multiple_of(position & -128, 128)
                near = ints[s, :, pl.ds(base, 128)]
                far = ints[s, :, pl.ds(base + 128, 128)]
                moved = turn(near, far, position, inner_of(slot), lanes)
                value = jnp.where(mine == g, moved, value)
            turned.append(value)
            at = s * (FULL + 128)
            if slot:
                tile = jnp.where(lanes < inner_of(slot), turned[slot - 1], value)
                packed[:, pl.ds(at + (slot - 1) * 128, 128)] = tile
            if s == 1 and slot == 4:
                send(FULL + 128, 4 * 128)
        if s == 0:
            held = turned[7]
            send(0, FULL)
        else:
            packed[:, pl.ds(FULL, 128)] = jnp.where(
                lanes < HALF, held, pltpu.roll(turned[7], HALF, axis=1)
            )
            send(FULL, 128)
            send(FULL + 5 * 128, 3 * 128)
    for copy in sends:
        copy.wait()


def pack(where_am_i, integrals_t, vir_irrep):
    anywhere = pl.BlockSpec(memory_space=pl.ANY)
    return pl.pallas_call(
        functools.partial(pack_kernel, where_am_i),
        in_specs=[anywhere, anywhere],
        out_specs=anywhere,
        out_shape=jax.ShapeDtypeStruct((8, COLS, PACK), jnp.float32),
        scratch_shapes=[
            pltpu.SMEM((NV,), jnp.int32),
            pltpu.SMEM((IRREPS + 1,), jnp.int32),
            pltpu.VMEM((2, COLS, WIDE), jnp.float32),
            pltpu.VMEM((2, COLS, CD), jnp.float32),
            pltpu.VMEM((COLS, PACK), jnp.float32),
            pltpu.SemaphoreType.DMA((5 + 32,)),
        ],
        compiler_params=pltpu.CompilerParams(vmem_limit_bytes=ALL_VMEM),
        name="pack",
    )(vir_irrep, integrals_t)


def pack_tau(o, v, vir_ref, occ_ref, vstart, ostart, amp_ref, singles_ref, amps, ones, single_win, left, group, high, low):
    c_first, offset = first_pair(v)
    for t in range(CD // 128 + 1):
        size = min(128, CD - t * 128)
        amps[LEAD // 128 + t, pl.ds(0, ROWS_I * NO), pl.ds(0, size)] = amp_ref[:, pl.ds(t * 128, size)]
    amps[:, pl.ds(ROWS_I * NO, 16), :] = jnp.zeros((WIDE // 128, 16, 128), jnp.float32)

    ones[...] = jnp.zeros_like(ones)
    for t in range(4):
        size = min(128, NV - t * 128)
        ones[t, pl.ds(0, NO), pl.ds(0, size)] = singles_ref[:, pl.ds(t * 128, size)]
    lanes_w = lax.broadcasted_iota(jnp.int32, (16, 128), 1)
    for g in range(IRREPS):
        at, rows = vstart[g], pl.ds(ostart[g], 16)
        single_win[g] = turn(ones[at >> 7, rows, :], ones[(at >> 7) + 1, rows, :], at, 0, lanes_w)
    lane_c = lax.broadcasted_iota(jnp.int32, (8, 128), 1)
    row_i = lax.broadcasted_iota(jnp.int32, (8, 1), 0)
    irr_i = [occ_ref[o * ROWS_I + i] for i in range(ROWS_I)]
    for slot in range(SLOTS):
        c = c_first + slot
        irr_c = vir_ref[c]
        own = ones[c >> 7, pl.ds(o * ROWS_I, 8), :]
        column = jnp.sum(jnp.where(lane_c == (c & 127), own, 0.0), axis=1, keepdims=True)
        for i in range(ROWS_I):
            column = jnp.where((row_i == i) & (irr_i[i] != irr_c), 0.0, column)
        left[slot] = jnp.broadcast_to(column, (8, 128))

    lanes = lax.broadcasted_iota(jnp.int32, (RUN_O, 128), 1)
    for sym in range(IRREPS):
        turned = [[] for _ in range(ROWS_I)]
        for slot in range(SLOTS):
            g = vir_ref[c_first + slot] ^ sym
            begin = slot * NV + vstart[g] - offset
            from_lane = jnp.maximum(0, -begin)
            to_lane = jnp.minimum(vstart[g + 1] - vstart[g], CD - begin)
            inner = inner_of(slot)
            k = (lanes + (128 - inner)) & 127
            keep = (k >= from_lane) & (k < to_lane)
            near = (LEAD + begin) >> 7
            right = pltpu.roll(single_win[g], inner, axis=1)[:RUN_O]
            for i in range(ROWS_I):
                rows = pl.ds(i * NO + ostart[irr_i[i] ^ sym], RUN_O)
                value = turn(amps[near, rows, :], amps[near + 1, rows, :], LEAD + begin, inner, lanes)
                product = left[slot, pl.ds(i, 1), :] * right
                turned[i].append(jnp.where(keep, value + product, 0.0))
        for i in range(ROWS_I):
            for t, tile in enumerate(tiles_of(turned[i], lanes)):
                if t == 7:
                    tile = jnp.where(lanes < HALF, tile, 0.0)
                group[pl.ds(sym * GROUP + i * RUN_O, RUN_O), pl.ds(t * 128, 128)] = tile
    wide = group[:, pl.ds(0, FULL)]
    top = wide.astype(jnp.bfloat16)
    high[:, pl.ds(0, FULL)] = top
    low[...] = (wide - top.astype(jnp.float32)).astype(jnp.bfloat16)
    last = group[:, pl.ds(FULL, 128)]
    upper = last.astype(jnp.bfloat16).astype(jnp.float32)
    lanes_all = lax.broadcasted_iota(jnp.int32, last.shape, 1)
    last = jnp.where(lanes_all < HALF, upper, pltpu.roll(last - upper, HALF, axis=1))
    high[:, pl.ds(FULL, 128)] = last.astype(jnp.bfloat16)


def spread_index(o, u, vir_ref, occ_ref, owner_ref, vlow, olow):
    block = jnp.int32(0)
    for k in range(64):
        block += jnp.where(owner_ref[k] == u, k, 0)
    lanes = lax.broadcasted_iota(jnp.int32, (8, 256), 1)
    row = lax.broadcasted_iota(jnp.int32, (8, 256), 0)
    column = jnp.where(row >= 4, SPAN - 4, 0) + block * 4 + row
    second = column >= NV
    sym = irrep_of(jnp.where(second, column - NV, column), vlow)
    sym = sym ^ jnp.where(second, vir_ref[1], vir_ref[0])
    i = jnp.zeros_like(lanes)
    irr_i = jnp.zeros_like(lanes)
    for n in range(ROWS_I):
        i = jnp.where(lanes >= n * NO, n, i)
        irr_i = jnp.where(lanes >= n * NO, occ_ref[o * ROWS_I + n], irr_i)
    j = lanes - i * NO
    irr_j = irrep_of(j, olow)
    begin = jnp.zeros_like(lanes)
    for g in range(1, IRREPS):
        begin = jnp.where(irr_j == g, olow[g], begin)
    lane = i * RUN_O + j - begin + jnp.where(row >= 4, HALF, 0)
    return jnp.where((sym ^ irr_i ^ irr_j) == 0, lane, -1)


def tau_kernel(
    where_am_i,
    vir_ref,
    occ_ref,
    owner_ref,
    amp_ref,
    singles_ref,
    high,
    low,
    index_ref,
    vstart,
    ostart,
    amps,
    ones,
    single_win,
    left,
    group,
):
    o, v = where_am_i()
    vlow = fill_starts(vir_ref, NV, vstart)
    olow = fill_starts(occ_ref, NO, ostart)
    pack_tau(o, v, vir_ref, occ_ref, vstart, ostart, amp_ref, singles_ref, amps, ones, single_win, left, group, high, low)
    index_ref[...] = spread_index(o, v, vir_ref, occ_ref, owner_ref, vlow, olow)


def tau(where_am_i, amplitudes, singles, occ_irrep, vir_irrep, owner):
    smem = pl.BlockSpec(memory_space=pltpu.SMEM)
    vmem = pl.BlockSpec(memory_space=pltpu.VMEM)
    depth = SLOTS * 128
    return pl.pallas_call(
        functools.partial(tau_kernel, where_am_i),
        in_specs=[smem, smem, smem, vmem, vmem],
        out_specs=[vmem, vmem, vmem],
        out_shape=[
            jax.ShapeDtypeStruct((IRREPS * GROUP, depth), jnp.bfloat16),
            jax.ShapeDtypeStruct((IRREPS * GROUP, FULL), jnp.bfloat16),
            jax.ShapeDtypeStruct((8, 256), jnp.int32),
        ],
        scratch_shapes=[
            pltpu.SMEM((IRREPS + 1,), jnp.int32),
            pltpu.SMEM((IRREPS + 1,), jnp.int32),
            pltpu.VMEM((WIDE // 128, ROWS_I * NO + 16, 128), jnp.float32),
            pltpu.VMEM((5, NO + 16, 128), jnp.float32),
            pltpu.VMEM((IRREPS, 16, 128), jnp.float32),
            pltpu.VMEM((SLOTS, 8, 128), jnp.float32),
            pltpu.VMEM((IRREPS * GROUP, depth), jnp.float32),
        ],
        compiler_params=pltpu.CompilerParams(vmem_limit_bytes=SOME_VMEM),
        cost_estimate=pl.CostEstimate(flops=0, bytes_accessed=8 * 1024 * 1024, transcendentals=0),
        name="tau",
    )(vir_irrep, occ_irrep, owner, amplitudes, singles)


def ladder_kernel(
    where_am_i, vir_ref, owner_ref, packed_ref, high, low, keep_ref, send_ref, vstart, top, bottom, sums, both_cores
):
    core = where_am_i()[1] & 1
    vlow = fill_starts(vir_ref, NV, vstart)
    lanes = lax.broadcasted_iota(jnp.int32, (COLS, 128), 1)
    contract = functools.partial(
        lax.dot_general,
        dimension_numbers=(((1,), (1,)), ((), ())),
        preferred_element_type=jnp.float32,
    )
    used = IRREPS * GROUP
    sums[pl.ds(used, 8), :] = jnp.zeros((8, 2 * SPAN), jnp.float32)

    def split(s):
        for source in range(8):
            last = packed_ref[source, :, pl.ds(FULL, 128)]
            other = pltpu.roll(last, HALF, axis=1)
            rows = pl.ds(s * SPAN + source * COLS, COLS)
            wide = packed_ref[source, :, pl.ds(s * (FULL + 128), FULL)]
            upper = wide.astype(jnp.bfloat16)
            top[rows, pl.ds(0, FULL)] = upper
            bottom[rows, pl.ds(0, FULL)] = (wide - upper.astype(jnp.float32)).astype(jnp.bfloat16)
            twice = jnp.where(lanes < HALF, last, other) if s == 0 else jnp.where(lanes < HALF, other, last)
            upper = twice.astype(jnp.bfloat16)
            top[rows, pl.ds(FULL, 128)] = upper
            rest = jnp.where(lanes < HALF, twice - upper.astype(jnp.float32), 0.0)
            bottom[rows, pl.ds(FULL, 128)] = rest.astype(jnp.bfloat16)

    def multiply(s):
        there = pl.ds(s * SPAN, SPAN)
        sums[pl.ds(0, used), there] = (
            contract(high[...], top[there, :])
            + contract(high[...], bottom[there, :])
            + contract(low[...], top[there, pl.ds(0, FULL)])
        )

    def pick(s):
        there = pl.ds(s * SPAN, SPAN)
        column = lax.broadcasted_iota(jnp.int32, (1, SPAN), 1) + s * SPAN
        second = column >= NV
        sym = irrep_of(jnp.where(second, column - NV, column), vlow)
        sym = sym ^ jnp.where(second, vir_ref[1], vir_ref[0])
        picked = sums[pl.ds(0, 56), there]
        for g in range(1, IRREPS):
            picked = jnp.where(sym == g, sums[pl.ds(g * GROUP, 56), there], picked)
        return picked

    split(0)
    multiply(0)
    split(1)
    multiply(1)
    pad = jnp.zeros((HALF - 56, SPAN), jnp.float32)
    both = 0.5 * jnp.transpose(jnp.concatenate([pick(0), pad, pick(1), pad], axis=0))
    for k in range(64):
        u = owner_ref[k]
        both_cores[(u & 1) ^ core, u >> 1] = both[4 * k : 4 * k + 4, :]
    keep_ref[...] = both_cores[0]
    send_ref[...] = both_cores[1]


def ladder(where_am_i, packed, high, low, vir_irrep, owner):
    smem = pl.BlockSpec(memory_space=pltpu.SMEM)
    vmem = pl.BlockSpec(memory_space=pltpu.VMEM)
    depth = SLOTS * 128
    return pl.pallas_call(
        functools.partial(ladder_kernel, where_am_i),
        in_specs=[smem, smem, vmem, vmem, vmem],
        out_specs=[vmem, vmem],
        out_shape=[jax.ShapeDtypeStruct((32, 4, 128), jnp.float32)] * 2,
        scratch_shapes=[
            pltpu.SMEM((IRREPS + 1,), jnp.int32),
            pltpu.VMEM((2 * SPAN, depth), jnp.bfloat16),
            pltpu.VMEM((2 * SPAN, depth), jnp.bfloat16),
            pltpu.VMEM((IRREPS * GROUP + 8, 2 * SPAN), jnp.float32),
            pltpu.VMEM((2, 32, 4, 128), jnp.float32),
        ],
        compiler_params=pltpu.CompilerParams(vmem_limit_bytes=SOME_VMEM),
        name="ladder",
    )(vir_irrep, owner, packed, high, low)


def finish_kernel(parts_ref, index_ref, out_ref):
    total = jnp.sum(parts_ref[...], axis=0)
    both = jnp.concatenate([total, total], axis=0)
    index = index_ref[...]
    lane = jnp.maximum(index, 0)
    near = jnp.take_along_axis(both, lane[:, :128], axis=1)
    far = jnp.take_along_axis(both, lane[:, 128:], axis=1)
    result = jnp.where(index >= 0, jnp.concatenate([near, far], axis=1), 0.0)
    out_ref[...] = result[:, : ROWS_I * NO]


def finish(parts, index):
    vmem = pl.BlockSpec(memory_space=pltpu.VMEM)
    return pl.pallas_call(
        finish_kernel,
        in_specs=[vmem, vmem],
        out_specs=vmem,
        out_shape=jax.ShapeDtypeStruct((8, ROWS_I * NO), jnp.float32),
        compiler_params=pltpu.CompilerParams(vmem_limit_bytes=1024 * 1024),
        name="finish",
    )(parts, index)


def shards(amplitudes, singles, integrals, occ_irrep, vir_irrep, owner):
    packed = pack(placed, jnp.transpose(integrals, (0, 2, 1)), vir_irrep)
    gathered = lax.all_to_all(packed, "occ", 0, 0, tiled=True)
    high, low, index = tau(placed, amplitudes, singles, occ_irrep, vir_irrep, owner)
    keep, send = ladder(placed, gathered, high, low, vir_irrep, owner)
    keep += lax.ppermute(send, "vir", [(n, n ^ 1) for n in range(64)])
    same_core = [list(range(core, 64, 2)) for core in range(2)]
    parts = lax.all_to_all(keep, "vir", 0, 0, axis_index_groups=same_core, tiled=True)
    return jnp.transpose(finish(parts, index))


def solution(mesh):
    specs = (P("occ", "vir"), P(), P(None, "vir", "occ"), P(), P(), P())
    return jax.shard_map(
        shards, mesh=mesh, in_specs=specs, out_specs=P("occ", "vir"), check_vma=False
    )
```

```python
import functools

import jax
import jax.numpy as jnp
from jax import lax
from jax.experimental import pallas as pl
from jax.experimental.pallas import tpu as pltpu
from jax.sharding import PartitionSpec as P

NO = 40
NV = 480
SPAN = 256
IRREPS = 8
RUN_V = 120
RUN_O = 10
ROWS_I = 5
COLS = 32
CD = 3600
SLOTS = 8
LEAD = 256
WIDE = 33 * 128
MAIN = 28 * 128
GROUP = 50
PACK = 2 * SLOTS * RUN_V
ALL_VMEM = 64 * 1024 * 1024
SOME_VMEM = 12 * 1024 * 1024
FULL = 7 * 128
HALF = 64


def placed():
    return lax.axis_index("occ"), lax.axis_index("vir")


def fill_starts(labels, length, starts):
    bit = 1
    while bit * 2 <= length:
        bit *= 2
    low = [jnp.int32(0)] * IRREPS
    while bit:
        for g in range(1, IRREPS):
            cand = low[g] + bit
            below = labels[jnp.minimum(cand, length) - 1] < g
            low[g] = jnp.where(below, cand, low[g])
        bit //= 2
    for g in range(IRREPS):
        starts[g] = low[g]
    starts[IRREPS] = jnp.int32(length)
    return low


def irrep_of(index, low):
    total = jnp.zeros_like(index)
    for g in range(1, IRREPS):
        total += (index >= low[g]).astype(jnp.int32)
    return total


def turn(near, far, position, inner, lanes):
    shift = position & 127
    amount = (inner + 128 - shift) & 127
    return pltpu.roll(jnp.where(lanes >= shift, near, far), amount, axis=1)


def inner_of(slot):
    return slot * RUN_V % 128


def tiles_of(turned, lanes):
    for slot in range(SLOTS - 1):
        yield jnp.where(lanes < inner_of(slot + 1), turned[slot], turned[slot + 1])
    yield turned[SLOTS - 1]


def first_pair(v):
    return (v * 15) >> 1, (v & 1) * (NV // 2)


def pack_kernel(where_am_i, vir_hbm, int_hbm, out_hbm, labels, starts, ints, whole, packed, sems):
    label_copy = pltpu.make_async_copy(vir_hbm, labels, sems.at[0])
    label_copy.start()
    copies = []
    for s in range(2):
        copies.append(
            [
                pltpu.make_async_copy(int_hbm.at[s], whole.at[s], sems.at[2 + 2 * s]),
            ]
        )
        for copy in copies[s]:
            copy.start()
    o, v = where_am_i()
    c_first, offset = first_pair(v)
    rest = WIDE - LEAD - MAIN - 128
    ints[:, :, pl.ds(0, LEAD)] = jnp.zeros((2, COLS, LEAD), jnp.float32)
    ints[:, :, pl.ds(LEAD + MAIN, 128)] = jnp.zeros((2, COLS, 128), jnp.float32)
    ints[:, :, pl.ds(LEAD + MAIN + 128, rest)] = jnp.zeros((2, COLS, rest), jnp.float32)
    label_copy.wait()
    low = fill_starts(labels, NV, starts)

    lanes = lax.broadcasted_iota(jnp.int32, (COLS, 128), 1)
    row = lax.broadcasted_iota(jnp.int32, (COLS, 128), 0)
    sends = []

    def send(at, size):
        for n in range(8):
            copy = pltpu.make_async_copy(
                packed.at[:, pl.ds(at, size)],
                out_hbm.at[n, :, pl.ds(at, size)],
                sems.at[5 + len(sends)],
            )
            copy.start()
            sends.append(copy)

    held = None
    irr_c = [labels[c_first + slot] for slot in range(SLOTS)]
    begin = [LEAD - offset + low[g] for g in range(IRREPS)]
    for s in range(2):
        for copy in copies[s]:
            copy.wait()
        ints[s, :, pl.ds(LEAD, CD)] = whole[s]
        first = s * SPAN + o * COLS
        a = (first >= NV).astype(jnp.int32)
        b = first - a * NV
        irr_a = labels[a]
        irr_b = irrep_of(row + b, low)
        turned = []
        for slot in range(SLOTS):
            cross = irr_c[slot] ^ irr_a
            mine = irr_b ^ cross
            value = jnp.zeros((COLS, 128), jnp.float32)
            for g in range(IRREPS):
                position = begin[g] + slot * NV
                base = pl.multiple_of(position & -128, 128)
                near = ints[s, :, pl.ds(base, 128)]
                far = ints[s, :, pl.ds(base + 128, 128)]
                moved = turn(near, far, position, inner_of(slot), lanes)
                value = jnp.where(mine == g, moved, value)
            turned.append(value)
            at = s * (FULL + 128)
            if slot:
                tile = jnp.where(lanes < inner_of(slot), turned[slot - 1], value)
                packed[:, pl.ds(at + (slot - 1) * 128, 128)] = tile
            if s == 1 and slot == 4:
                send(FULL + 128, 4 * 128)
        if s == 0:
            held = turned[7]
            send(0, FULL)
        else:
            packed[:, pl.ds(FULL, 128)] = jnp.where(
                lanes < HALF, held, pltpu.roll(turned[7], HALF, axis=1)
            )
            send(FULL, 128)
            send(FULL + 5 * 128, 3 * 128)
    for copy in sends:
        copy.wait()


def pack(where_am_i, integrals_t, vir_irrep):
    anywhere = pl.BlockSpec(memory_space=pl.ANY)
    return pl.pallas_call(
        functools.partial(pack_kernel, where_am_i),
        in_specs=[anywhere, anywhere],
        out_specs=anywhere,
        out_shape=jax.ShapeDtypeStruct((8, COLS, PACK), jnp.float32),
        scratch_shapes=[
            pltpu.SMEM((NV,), jnp.int32),
            pltpu.SMEM((IRREPS + 1,), jnp.int32),
            pltpu.VMEM((2, COLS, WIDE), jnp.float32),
            pltpu.VMEM((2, COLS, CD), jnp.float32),
            pltpu.VMEM((COLS, PACK), jnp.float32),
            pltpu.SemaphoreType.DMA((5 + 32,)),
        ],
        compiler_params=pltpu.CompilerParams(vmem_limit_bytes=ALL_VMEM),
        name="pack",
    )(vir_irrep, integrals_t)


def pack_tau(o, v, vir_ref, occ_ref, vstart, ostart, amp_ref, singles_ref, amps, ones, single_win, left, group, high, low):
    c_first, offset = first_pair(v)
    for t in range(CD // 128 + 1):
        size = min(128, CD - t * 128)
        amps[LEAD // 128 + t, pl.ds(0, ROWS_I * NO), pl.ds(0, size)] = amp_ref[:, pl.ds(t * 128, size)]
    amps[:, pl.ds(ROWS_I * NO, 16), :] = jnp.zeros((WIDE // 128, 16, 128), jnp.float32)

    ones[...] = jnp.zeros_like(ones)
    for t in range(4):
        size = min(128, NV - t * 128)
        ones[t, pl.ds(0, NO), pl.ds(0, size)] = singles_ref[:, pl.ds(t * 128, size)]
    lanes_w = lax.broadcasted_iota(jnp.int32, (16, 128), 1)
    for g in range(IRREPS):
        at, rows = vstart[g], pl.ds(ostart[g], 16)
        single_win[g] = turn(ones[at >> 7, rows, :], ones[(at >> 7) + 1, rows, :], at, 0, lanes_w)
    lane_c = lax.broadcasted_iota(jnp.int32, (8, 128), 1)
    row_i = lax.broadcasted_iota(jnp.int32, (8, 1), 0)
    irr_i = [occ_ref[o * ROWS_I + i] for i in range(ROWS_I)]
    for slot in range(SLOTS):
        c = c_first + slot
        irr_c = vir_ref[c]
        own = ones[c >> 7, pl.ds(o * ROWS_I, 8), :]
        column = jnp.sum(jnp.where(lane_c == (c & 127), own, 0.0), axis=1, keepdims=True)
        for i in range(ROWS_I):
            column = jnp.where((row_i == i) & (irr_i[i] != irr_c), 0.0, column)
        left[slot] = jnp.broadcast_to(column, (8, 128))

    lanes = lax.broadcasted_iota(jnp.int32, (RUN_O, 128), 1)
    for sym in range(IRREPS):
        turned = [[] for _ in range(ROWS_I)]
        for slot in range(SLOTS):
            g = vir_ref[c_first + slot] ^ sym
            begin = slot * NV + vstart[g] - offset
            from_lane = jnp.maximum(0, -begin)
            to_lane = jnp.minimum(vstart[g + 1] - vstart[g], CD - begin)
            inner = inner_of(slot)
            k = (lanes + (128 - inner)) & 127
            keep = (k >= from_lane) & (k < to_lane)
            near = (LEAD + begin) >> 7
            right = pltpu.roll(single_win[g], inner, axis=1)[:RUN_O]
            for i in range(ROWS_I):
                rows = pl.ds(i * NO + ostart[irr_i[i] ^ sym], RUN_O)
                value = turn(amps[near, rows, :], amps[near + 1, rows, :], LEAD + begin, inner, lanes)
                product = left[slot, pl.ds(i, 1), :] * right
                turned[i].append(jnp.where(keep, value + product, 0.0))
        for i in range(ROWS_I):
            for t, tile in enumerate(tiles_of(turned[i], lanes)):
                if t == 7:
                    tile = jnp.where(lanes < HALF, tile, 0.0)
                group[pl.ds(sym * GROUP + i * RUN_O, RUN_O), pl.ds(t * 128, 128)] = tile
    wide = group[:, pl.ds(0, FULL)]
    top = wide.astype(jnp.bfloat16)
    high[:, pl.ds(0, FULL)] = top
    low[...] = (wide - top.astype(jnp.float32)).astype(jnp.bfloat16)
    last = group[:, pl.ds(FULL, 128)]
    upper = last.astype(jnp.bfloat16).astype(jnp.float32)
    lanes_all = lax.broadcasted_iota(jnp.int32, last.shape, 1)
    last = jnp.where(lanes_all < HALF, upper, pltpu.roll(last - upper, HALF, axis=1))
    high[:, pl.ds(FULL, 128)] = last.astype(jnp.bfloat16)


def spread_index(o, u, vir_ref, occ_ref, owner_ref, vlow, olow):
    block = jnp.int32(0)
    for k in range(64):
        block += jnp.where(owner_ref[k] == u, k, 0)
    lanes = lax.broadcasted_iota(jnp.int32, (8, 256), 1)
    row = lax.broadcasted_iota(jnp.int32, (8, 256), 0)
    column = jnp.where(row >= 4, SPAN - 4, 0) + block * 4 + row
    second = column >= NV
    sym = irrep_of(jnp.where(second, column - NV, column), vlow)
    sym = sym ^ jnp.where(second, vir_ref[1], vir_ref[0])
    i = jnp.zeros_like(lanes)
    irr_i = jnp.zeros_like(lanes)
    for n in range(ROWS_I):
        i = jnp.where(lanes >= n * NO, n, i)
        irr_i = jnp.where(lanes >= n * NO, occ_ref[o * ROWS_I + n], irr_i)
    j = lanes - i * NO
    irr_j = irrep_of(j, olow)
    begin = jnp.zeros_like(lanes)
    for g in range(1, IRREPS):
        begin = jnp.where(irr_j == g, olow[g], begin)
    lane = i * RUN_O + j - begin + jnp.where(row >= 4, HALF, 0)
    wanted = ((sym ^ irr_i ^ irr_j) == 0) & (lanes < ROWS_I * NO)
    return jnp.where(wanted, lane, -1)


def tau_kernel(
    where_am_i,
    vir_ref,
    occ_ref,
    owner_ref,
    amp_ref,
    singles_ref,
    high,
    low,
    index_ref,
    vstart,
    ostart,
    amps,
    ones,
    single_win,
    left,
    group,
):
    o, v = where_am_i()
    vlow = fill_starts(vir_ref, NV, vstart)
    olow = fill_starts(occ_ref, NO, ostart)
    pack_tau(o, v, vir_ref, occ_ref, vstart, ostart, amp_ref, singles_ref, amps, ones, single_win, left, group, high, low)
    index_ref[...] = spread_index(o, v, vir_ref, occ_ref, owner_ref, vlow, olow)


def tau(where_am_i, amplitudes, singles, occ_irrep, vir_irrep, owner):
    smem = pl.BlockSpec(memory_space=pltpu.SMEM)
    vmem = pl.BlockSpec(memory_space=pltpu.VMEM)
    depth = SLOTS * 128
    return pl.pallas_call(
        functools.partial(tau_kernel, where_am_i),
        in_specs=[smem, smem, smem, vmem, vmem],
        out_specs=[vmem, vmem, vmem],
        out_shape=[
            jax.ShapeDtypeStruct((IRREPS * GROUP, depth), jnp.bfloat16),
            jax.ShapeDtypeStruct((IRREPS * GROUP, FULL), jnp.bfloat16),
            jax.ShapeDtypeStruct((8, 256), jnp.int32),
        ],
        scratch_shapes=[
            pltpu.SMEM((IRREPS + 1,), jnp.int32),
            pltpu.SMEM((IRREPS + 1,), jnp.int32),
            pltpu.VMEM((WIDE // 128, ROWS_I * NO + 16, 128), jnp.float32),
            pltpu.VMEM((5, NO + 16, 128), jnp.float32),
            pltpu.VMEM((IRREPS, 16, 128), jnp.float32),
            pltpu.VMEM((SLOTS, 8, 128), jnp.float32),
            pltpu.VMEM((IRREPS * GROUP, depth), jnp.float32),
        ],
        compiler_params=pltpu.CompilerParams(vmem_limit_bytes=SOME_VMEM),
        cost_estimate=pl.CostEstimate(flops=0, bytes_accessed=8 * 1024 * 1024, transcendentals=0),
        name="tau",
    )(vir_irrep, occ_irrep, owner, amplitudes, singles)


def ladder_kernel(
    where_am_i, vir_ref, owner_ref, packed_ref, high, low, keep_ref, send_ref, vstart, top, bottom, sums, both_cores
):
    core = where_am_i()[1] & 1
    vlow = fill_starts(vir_ref, NV, vstart)
    lanes = lax.broadcasted_iota(jnp.int32, (COLS, 128), 1)
    contract = functools.partial(
        lax.dot_general,
        dimension_numbers=(((1,), (1,)), ((), ())),
        preferred_element_type=jnp.float32,
    )
    used = IRREPS * GROUP
    sums[pl.ds(used, 8), :] = jnp.zeros((8, 2 * SPAN), jnp.float32)

    def split(s):
        for source in range(8):
            last = packed_ref[source, :, pl.ds(FULL, 128)]
            other = pltpu.roll(last, HALF, axis=1)
            rows = pl.ds(s * SPAN + source * COLS, COLS)
            wide = packed_ref[source, :, pl.ds(s * (FULL + 128), FULL)]
            upper = wide.astype(jnp.bfloat16)
            top[rows, pl.ds(0, FULL)] = upper
            bottom[rows, pl.ds(0, FULL)] = (wide - upper.astype(jnp.float32)).astype(jnp.bfloat16)
            twice = jnp.where(lanes < HALF, last, other) if s == 0 else jnp.where(lanes < HALF, other, last)
            upper = twice.astype(jnp.bfloat16)
            top[rows, pl.ds(FULL, 128)] = upper
            rest = jnp.where(lanes < HALF, twice - upper.astype(jnp.float32), 0.0)
            bottom[rows, pl.ds(FULL, 128)] = rest.astype(jnp.bfloat16)

    def multiply(s):
        there = pl.ds(s * SPAN, SPAN)
        sums[pl.ds(0, used), there] = (
            contract(high[...], top[there, :])
            + contract(high[...], bottom[there, :])
            + contract(low[...], top[there, pl.ds(0, FULL)])
        )

    def pick(s):
        there = pl.ds(s * SPAN, SPAN)
        column = lax.broadcasted_iota(jnp.int32, (1, SPAN), 1) + s * SPAN
        second = column >= NV
        sym = irrep_of(jnp.where(second, column - NV, column), vlow)
        sym = sym ^ jnp.where(second, vir_ref[1], vir_ref[0])
        picked = sums[pl.ds(0, 56), there]
        for g in range(1, IRREPS):
            picked = jnp.where(sym == g, sums[pl.ds(g * GROUP, 56), there], picked)
        return picked

    split(0)
    multiply(0)
    split(1)
    multiply(1)
    pad = jnp.zeros((HALF - 56, SPAN), jnp.float32)
    both = 0.5 * jnp.transpose(jnp.concatenate([pick(0), pad, pick(1), pad], axis=0))
    for k in range(64):
        u = owner_ref[k]
        both_cores[(u & 1) ^ core, u >> 1] = both[4 * k : 4 * k + 4, :]
    keep_ref[...] = both_cores[0]
    send_ref[...] = both_cores[1]


def ladder(where_am_i, packed, high, low, vir_irrep, owner):
    smem = pl.BlockSpec(memory_space=pltpu.SMEM)
    vmem = pl.BlockSpec(memory_space=pltpu.VMEM)
    depth = SLOTS * 128
    return pl.pallas_call(
        functools.partial(ladder_kernel, where_am_i),
        in_specs=[smem, smem, vmem, vmem, vmem],
        out_specs=[vmem, vmem],
        out_shape=[jax.ShapeDtypeStruct((32, 4, 128), jnp.float32)] * 2,
        scratch_shapes=[
            pltpu.SMEM((IRREPS + 1,), jnp.int32),
            pltpu.VMEM((2 * SPAN, depth), jnp.bfloat16),
            pltpu.VMEM((2 * SPAN, depth), jnp.bfloat16),
            pltpu.VMEM((IRREPS * GROUP + 8, 2 * SPAN), jnp.float32),
            pltpu.VMEM((2, 32, 4, 128), jnp.float32),
        ],
        compiler_params=pltpu.CompilerParams(vmem_limit_bytes=SOME_VMEM),
        name="ladder",
    )(vir_irrep, owner, packed, high, low)


def finish_kernel(parts_ref, index_ref, out_ref):
    total = jnp.sum(parts_ref[...], axis=0)
    both = jnp.concatenate([total, total], axis=0)
    index = index_ref[...]
    lane = jnp.maximum(index, 0)
    near = jnp.take_along_axis(both, lane[:, :128], axis=1)
    far = jnp.take_along_axis(both, lane[:, 128:], axis=1)
    result = jnp.where(index >= 0, jnp.concatenate([near, far], axis=1), 0.0)
    out_ref[...] = result[:, : ROWS_I * NO]


def finish(parts, index):
    vmem = pl.BlockSpec(memory_space=pltpu.VMEM)
    return pl.pallas_call(
        finish_kernel,
        in_specs=[vmem, vmem],
        out_specs=vmem,
        out_shape=jax.ShapeDtypeStruct((8, ROWS_I * NO), jnp.float32),
        compiler_params=pltpu.CompilerParams(vmem_limit_bytes=1024 * 1024),
        name="finish",
    )(parts, index)


def shards(amplitudes, singles, integrals, occ_irrep, vir_irrep, owner):
    packed = pack(placed, jnp.transpose(integrals, (0, 2, 1)), vir_irrep)
    gathered = lax.all_to_all(packed, "occ", 0, 0, tiled=True)
    high, low, index = tau(placed, amplitudes, singles, occ_irrep, vir_irrep, owner)
    keep, send = ladder(placed, gathered, high, low, vir_irrep, owner)
    keep += lax.ppermute(send, "vir", [(n, n ^ 1) for n in range(64)])
    same_core = [list(range(core, 64, 2)) for core in range(2)]
    parts = lax.all_to_all(keep, "vir", 0, 0, axis_index_groups=same_core, tiled=True)
    return jnp.transpose(finish(parts, index))


def solution(mesh):
    specs = (P("occ", "vir"), P(), P(None, "vir", "occ"), P(), P(), P())
    return jax.shard_map(
        shards, mesh=mesh, in_specs=specs, out_specs=P("occ", "vir"), check_vma=False
    )
```

```python
import functools

import jax
import jax.numpy as jnp
from jax import lax
from jax.experimental import pallas as pl
from jax.experimental.pallas import tpu as pltpu
from jax.sharding import PartitionSpec as P

NO = 40
NV = 480
SPAN = 256
IRREPS = 8
RUN_V = 120
RUN_O = 10
ROWS_I = 5
COLS = 32
CD = 3600
SLOTS = 8
LEAD = 256
WIDE = 33 * 128
MAIN = 28 * 128
GROUP = 50
PACK = 2 * SLOTS * RUN_V
ALL_VMEM = 64 * 1024 * 1024
SOME_VMEM = 12 * 1024 * 1024
FULL = 7 * 128
HALF = 64


def placed():
    return lax.axis_index("occ"), lax.axis_index("vir")


def fill_starts(labels, length, starts):
    bit = 1
    while bit * 2 <= length:
        bit *= 2
    low = [jnp.int32(0)] * IRREPS
    while bit:
        for g in range(1, IRREPS):
            cand = low[g] + bit
            below = labels[jnp.minimum(cand, length) - 1] < g
            low[g] = jnp.where(below, cand, low[g])
        bit //= 2
    for g in range(IRREPS):
        starts[g] = low[g]
    starts[IRREPS] = jnp.int32(length)
    return low


def irrep_of(index, low):
    total = jnp.zeros_like(index)
    for g in range(1, IRREPS):
        total += (index >= low[g]).astype(jnp.int32)
    return total


def turn(near, far, position, inner, lanes):
    shift = position & 127
    amount = (inner + 128 - shift) & 127
    return pltpu.roll(jnp.where(lanes >= shift, near, far), amount, axis=1)


def inner_of(slot):
    return slot * RUN_V % 128


def tiles_of(turned, lanes):
    for slot in range(SLOTS - 1):
        yield jnp.where(lanes < inner_of(slot + 1), turned[slot], turned[slot + 1])
    yield turned[SLOTS - 1]


def first_pair(v):
    return (v * 15) >> 1, (v & 1) * (NV // 2)


def pack_kernel(where_am_i, vir_hbm, int_hbm, out_hbm, labels, starts, ints, whole, packed, sems):
    label_copy = pltpu.make_async_copy(vir_hbm, labels, sems.at[0])
    label_copy.start()
    copies = []
    for s in range(2):
        copies.append(
            [
                pltpu.make_async_copy(int_hbm.at[s], whole.at[s], sems.at[2 + 2 * s]),
            ]
        )
        for copy in copies[s]:
            copy.start()
    o, v = where_am_i()
    c_first, offset = first_pair(v)
    rest = WIDE - LEAD - MAIN - 128
    ints[:, :, pl.ds(0, LEAD)] = jnp.zeros((2, COLS, LEAD), jnp.float32)
    ints[:, :, pl.ds(LEAD + MAIN, 128)] = jnp.zeros((2, COLS, 128), jnp.float32)
    ints[:, :, pl.ds(LEAD + MAIN + 128, rest)] = jnp.zeros((2, COLS, rest), jnp.float32)
    label_copy.wait()
    low = fill_starts(labels, NV, starts)

    lanes = lax.broadcasted_iota(jnp.int32, (COLS, 128), 1)
    row = lax.broadcasted_iota(jnp.int32, (COLS, 128), 0)
    sends = []

    def send(at, size):
        for n in range(8):
            copy = pltpu.make_async_copy(
                packed.at[:, pl.ds(at, size)],
                out_hbm.at[n, :, pl.ds(at, size)],
                sems.at[5 + len(sends)],
            )
            copy.start()
            sends.append(copy)

    held = None
    irr_c = [labels[c_first + slot] for slot in range(SLOTS)]
    begin = [LEAD - offset + low[g] for g in range(IRREPS)]
    for s in range(2):
        for copy in copies[s]:
            copy.wait()
        ints[s, :, pl.ds(LEAD, CD)] = whole[s]
        first = s * SPAN + o * COLS
        a = (first >= NV).astype(jnp.int32)
        b = first - a * NV
        irr_a = labels[a]
        irr_b = irrep_of(row + b, low)
        turned = []
        for slot in range(SLOTS):
            cross = irr_c[slot] ^ irr_a
            mine = irr_b ^ cross
            value = jnp.zeros((COLS, 128), jnp.float32)
            for g in range(IRREPS):
                position = begin[g] + slot * NV
                base = pl.multiple_of(position & -128, 128)
                near = ints[s, :, pl.ds(base, 128)]
                far = ints[s, :, pl.ds(base + 128, 128)]
                moved = turn(near, far, position, inner_of(slot), lanes)
                value = jnp.where(mine == g, moved, value)
            turned.append(value)
            at = s * (FULL + 128)
            if slot:
                tile = jnp.where(lanes < inner_of(slot), turned[slot - 1], value)
                packed[:, pl.ds(at + (slot - 1) * 128, 128)] = tile
            if s == 1 and slot == 4:
                send(FULL + 128, 4 * 128)
        if s == 0:
            held = turned[7]
            send(0, FULL)
        else:
            packed[:, pl.ds(FULL, 128)] = jnp.where(
                lanes < HALF, held, pltpu.roll(turned[7], HALF, axis=1)
            )
            send(FULL, 128)
            send(FULL + 5 * 128, 3 * 128)
    for copy in sends:
        copy.wait()


def pack(where_am_i, integrals_t, vir_irrep):
    anywhere = pl.BlockSpec(memory_space=pl.ANY)
    return pl.pallas_call(
        functools.partial(pack_kernel, where_am_i),
        in_specs=[anywhere, anywhere],
        out_specs=anywhere,
        out_shape=jax.ShapeDtypeStruct((8, COLS, PACK), jnp.float32),
        scratch_shapes=[
            pltpu.SMEM((NV,), jnp.int32),
            pltpu.SMEM((IRREPS + 1,), jnp.int32),
            pltpu.VMEM((2, COLS, WIDE), jnp.float32),
            pltpu.VMEM((2, COLS, CD), jnp.float32),
            pltpu.VMEM((COLS, PACK), jnp.float32),
            pltpu.SemaphoreType.DMA((5 + 32,)),
        ],
        compiler_params=pltpu.CompilerParams(vmem_limit_bytes=ALL_VMEM),
        name="pack",
    )(vir_irrep, integrals_t)


def pack_tau(o, v, vir_ref, occ_ref, vstart, ostart, amp_ref, singles_ref, amps, ones, single_win, left, group, high, low):
    c_first, offset = first_pair(v)
    for t in range(CD // 128 + 1):
        size = min(128, CD - t * 128)
        amps[LEAD // 128 + t, pl.ds(0, ROWS_I * NO), pl.ds(0, size)] = amp_ref[:, pl.ds(t * 128, size)]
    amps[:, pl.ds(ROWS_I * NO, 16), :] = jnp.zeros((WIDE // 128, 16, 128), jnp.float32)

    ones[...] = jnp.zeros_like(ones)
    for t in range(4):
        size = min(128, NV - t * 128)
        ones[t, pl.ds(0, NO), pl.ds(0, size)] = singles_ref[:, pl.ds(t * 128, size)]
    lanes_w = lax.broadcasted_iota(jnp.int32, (16, 128), 1)
    for g in range(IRREPS):
        at, rows = vstart[g], pl.ds(ostart[g], 16)
        single_win[g] = turn(ones[at >> 7, rows, :], ones[(at >> 7) + 1, rows, :], at, 0, lanes_w)
    lane_c = lax.broadcasted_iota(jnp.int32, (8, 128), 1)
    row_i = lax.broadcasted_iota(jnp.int32, (8, 1), 0)
    irr_i = [occ_ref[o * ROWS_I + i] for i in range(ROWS_I)]
    for slot in range(SLOTS):
        c = c_first + slot
        irr_c = vir_ref[c]
        own = ones[c >> 7, pl.ds(o * ROWS_I, 8), :]
        column = jnp.sum(jnp.where(lane_c == (c & 127), own, 0.0), axis=1, keepdims=True)
        for i in range(ROWS_I):
            column = jnp.where((row_i == i) & (irr_i[i] != irr_c), 0.0, column)
        left[slot] = jnp.broadcast_to(column, (8, 128))

    lanes = lax.broadcasted_iota(jnp.int32, (RUN_O, 128), 1)
    for sym in range(IRREPS):
        turned = [[] for _ in range(ROWS_I)]
        for slot in range(SLOTS):
            g = vir_ref[c_first + slot] ^ sym
            begin = slot * NV + vstart[g] - offset
            from_lane = jnp.maximum(0, -begin)
            to_lane = jnp.minimum(vstart[g + 1] - vstart[g], CD - begin)
            inner = inner_of(slot)
            k = (lanes + (128 - inner)) & 127
            keep = (k >= from_lane) & (k < to_lane)
            near = (LEAD + begin) >> 7
            right = pltpu.roll(single_win[g], inner, axis=1)[:RUN_O]
            for i in range(ROWS_I):
                rows = pl.ds(i * NO + ostart[irr_i[i] ^ sym], RUN_O)
                value = turn(amps[near, rows, :], amps[near + 1, rows, :], LEAD + begin, inner, lanes)
                product = left[slot, pl.ds(i, 1), :] * right
                turned[i].append(jnp.where(keep, value + product, 0.0))
        for i in range(ROWS_I):
            for t, tile in enumerate(tiles_of(turned[i], lanes)):
                if t == 7:
                    tile = jnp.where(lanes < HALF, tile, 0.0)
                group[pl.ds(sym * GROUP + i * RUN_O, RUN_O), pl.ds(t * 128, 128)] = tile
    wide = group[:, pl.ds(0, FULL)]
    top = wide.astype(jnp.bfloat16)
    high[:, pl.ds(0, FULL)] = top
    low[...] = (wide - top.astype(jnp.float32)).astype(jnp.bfloat16)
    last = group[:, pl.ds(FULL, 128)]
    upper = last.astype(jnp.bfloat16).astype(jnp.float32)
    lanes_all = lax.broadcasted_iota(jnp.int32, last.shape, 1)
    last = jnp.where(lanes_all < HALF, upper, pltpu.roll(last - upper, HALF, axis=1))
    high[:, pl.ds(FULL, 128)] = last.astype(jnp.bfloat16)


def spread_index(o, u, vir_ref, occ_ref, owner_ref, vlow, olow):
    block = jnp.int32(0)
    for k in range(64):
        block += jnp.where(owner_ref[k] == u, k, 0)
    lanes = lax.broadcasted_iota(jnp.int32, (8, 256), 1)
    row = lax.broadcasted_iota(jnp.int32, (8, 256), 0)
    column = jnp.where(row >= 4, SPAN - 4, 0) + block * 4 + row
    second = column >= NV
    sym = irrep_of(jnp.where(second, column - NV, column), vlow)
    sym = sym ^ jnp.where(second, vir_ref[1], vir_ref[0])
    i = jnp.zeros_like(lanes)
    irr_i = jnp.zeros_like(lanes)
    for n in range(ROWS_I):
        i = jnp.where(lanes >= n * NO, n, i)
        irr_i = jnp.where(lanes >= n * NO, occ_ref[o * ROWS_I + n], irr_i)
    j = lanes - i * NO
    irr_j = irrep_of(j, olow)
    begin = jnp.zeros_like(lanes)
    for g in range(1, IRREPS):
        begin = jnp.where(irr_j == g, olow[g], begin)
    lane = i * RUN_O + j - begin + jnp.where(row >= 4, HALF, 0)
    wanted = ((sym ^ irr_i ^ irr_j) == 0) & (lanes < ROWS_I * NO)
    return jnp.where(wanted, lane, -1)


def tau_kernel(
    where_am_i,
    vir_ref,
    occ_ref,
    owner_ref,
    amp_ref,
    singles_ref,
    high,
    low,
    index_ref,
    vstart,
    ostart,
    amps,
    ones,
    single_win,
    left,
    group,
):
    o, v = where_am_i()
    vlow = fill_starts(vir_ref, NV, vstart)
    olow = fill_starts(occ_ref, NO, ostart)
    pack_tau(o, v, vir_ref, occ_ref, vstart, ostart, amp_ref, singles_ref, amps, ones, single_win, left, group, high, low)
    index_ref[...] = spread_index(o, v, vir_ref, occ_ref, owner_ref, vlow, olow)


def tau(where_am_i, amplitudes, singles, occ_irrep, vir_irrep, owner):
    smem = pl.BlockSpec(memory_space=pltpu.SMEM)
    vmem = pl.BlockSpec(memory_space=pltpu.VMEM)
    depth = SLOTS * 128
    return pl.pallas_call(
        functools.partial(tau_kernel, where_am_i),
        in_specs=[smem, smem, smem, vmem, vmem],
        out_specs=[vmem, vmem, vmem],
        out_shape=[
            jax.ShapeDtypeStruct((IRREPS * GROUP, depth), jnp.bfloat16),
            jax.ShapeDtypeStruct((IRREPS * GROUP, FULL), jnp.bfloat16),
            jax.ShapeDtypeStruct((8, 256), jnp.int32),
        ],
        scratch_shapes=[
            pltpu.SMEM((IRREPS + 1,), jnp.int32),
            pltpu.SMEM((IRREPS + 1,), jnp.int32),
            pltpu.VMEM((WIDE // 128, ROWS_I * NO + 16, 128), jnp.float32),
            pltpu.VMEM((5, NO + 16, 128), jnp.float32),
            pltpu.VMEM((IRREPS, 16, 128), jnp.float32),
            pltpu.VMEM((SLOTS, 8, 128), jnp.float32),
            pltpu.VMEM((IRREPS * GROUP, depth), jnp.float32),
        ],
        compiler_params=pltpu.CompilerParams(vmem_limit_bytes=SOME_VMEM),
        cost_estimate=pl.CostEstimate(flops=0, bytes_accessed=8 * 1024 * 1024, transcendentals=0),
        name="tau",
    )(vir_irrep, occ_irrep, owner, amplitudes, singles)


def place_of(u):
    z = u >> 2
    return ((z & 7) << 2) | ((z >> 3) << 1) | ((u >> 1) & 1)


def ladder_kernel(
    where_am_i, vir_ref, owner_ref, packed_ref, high, low, keep_ref, send_ref, vstart, top, bottom, sums, both_cores
):
    core = where_am_i()[1] & 1
    vlow = fill_starts(vir_ref, NV, vstart)
    lanes = lax.broadcasted_iota(jnp.int32, (COLS, 128), 1)
    contract = functools.partial(
        lax.dot_general,
        dimension_numbers=(((1,), (1,)), ((), ())),
        preferred_element_type=jnp.float32,
    )
    used = IRREPS * GROUP
    sums[pl.ds(used, 8), :] = jnp.zeros((8, 2 * SPAN), jnp.float32)

    def split(s):
        for source in range(8):
            last = packed_ref[source, :, pl.ds(FULL, 128)]
            other = pltpu.roll(last, HALF, axis=1)
            rows = pl.ds(s * SPAN + source * COLS, COLS)
            wide = packed_ref[source, :, pl.ds(s * (FULL + 128), FULL)]
            upper = wide.astype(jnp.bfloat16)
            top[rows, pl.ds(0, FULL)] = upper
            bottom[rows, pl.ds(0, FULL)] = (wide - upper.astype(jnp.float32)).astype(jnp.bfloat16)
            twice = jnp.where(lanes < HALF, last, other) if s == 0 else jnp.where(lanes < HALF, other, last)
            upper = twice.astype(jnp.bfloat16)
            top[rows, pl.ds(FULL, 128)] = upper
            rest = jnp.where(lanes < HALF, twice - upper.astype(jnp.float32), 0.0)
            bottom[rows, pl.ds(FULL, 128)] = rest.astype(jnp.bfloat16)

    def multiply(s):
        there = pl.ds(s * SPAN, SPAN)
        sums[pl.ds(0, used), there] = (
            contract(high[...], top[there, :])
            + contract(high[...], bottom[there, :])
            + contract(low[...], top[there, pl.ds(0, FULL)])
        )

    def pick(s):
        there = pl.ds(s * SPAN, SPAN)
        column = lax.broadcasted_iota(jnp.int32, (1, SPAN), 1) + s * SPAN
        second = column >= NV
        sym = irrep_of(jnp.where(second, column - NV, column), vlow)
        sym = sym ^ jnp.where(second, vir_ref[1], vir_ref[0])
        picked = sums[pl.ds(0, 56), there]
        for g in range(1, IRREPS):
            picked = jnp.where(sym == g, sums[pl.ds(g * GROUP, 56), there], picked)
        return picked

    split(0)
    multiply(0)
    split(1)
    multiply(1)
    pad = jnp.zeros((HALF - 56, SPAN), jnp.float32)
    both = 0.5 * jnp.transpose(jnp.concatenate([pick(0), pad, pick(1), pad], axis=0))
    for k in range(64):
        u = owner_ref[k]
        both_cores[(u & 1) ^ core, place_of(u)] = both[4 * k : 4 * k + 4, :]
    keep_ref[...] = both_cores[0]
    send_ref[...] = both_cores[1]


def ladder(where_am_i, packed, high, low, vir_irrep, owner):
    smem = pl.BlockSpec(memory_space=pltpu.SMEM)
    vmem = pl.BlockSpec(memory_space=pltpu.VMEM)
    depth = SLOTS * 128
    return pl.pallas_call(
        functools.partial(ladder_kernel, where_am_i),
        in_specs=[smem, smem, vmem, vmem, vmem],
        out_specs=[vmem, vmem],
        out_shape=[jax.ShapeDtypeStruct((32, 4, 128), jnp.float32)] * 2,
        scratch_shapes=[
            pltpu.SMEM((IRREPS + 1,), jnp.int32),
            pltpu.VMEM((2 * SPAN, depth), jnp.bfloat16),
            pltpu.VMEM((2 * SPAN, depth), jnp.bfloat16),
            pltpu.VMEM((IRREPS * GROUP + 8, 2 * SPAN), jnp.float32),
            pltpu.VMEM((2, 32, 4, 128), jnp.float32),
        ],
        compiler_params=pltpu.CompilerParams(vmem_limit_bytes=SOME_VMEM),
        name="ladder",
    )(vir_irrep, owner, packed, high, low)


def finish_kernel(parts_ref, index_ref, out_ref):
    total = jnp.sum(parts_ref[...], axis=0)
    both = jnp.concatenate([total, total], axis=0)
    index = index_ref[...]
    lane = jnp.maximum(index, 0)
    near = jnp.take_along_axis(both, lane[:, :128], axis=1)
    far = jnp.take_along_axis(both, lane[:, 128:], axis=1)
    result = jnp.where(index >= 0, jnp.concatenate([near, far], axis=1), 0.0)
    out_ref[...] = result[:, : ROWS_I * NO]


def finish(parts, index):
    vmem = pl.BlockSpec(memory_space=pltpu.VMEM)
    return pl.pallas_call(
        finish_kernel,
        in_specs=[vmem, vmem],
        out_specs=vmem,
        out_shape=jax.ShapeDtypeStruct((8, ROWS_I * NO), jnp.float32),
        compiler_params=pltpu.CompilerParams(vmem_limit_bytes=1024 * 1024),
        name="finish",
    )(parts, index)


def shards(amplitudes, singles, integrals, occ_irrep, vir_irrep, owner):
    packed = pack(placed, jnp.transpose(integrals, (0, 2, 1)), vir_irrep)
    gathered = lax.all_to_all(packed, "occ", 0, 0, tiled=True)
    high, low, index = tau(placed, amplitudes, singles, occ_irrep, vir_irrep, owner)
    keep, send = ladder(placed, gathered, high, low, vir_irrep, owner)
    keep += lax.ppermute(send, "vir", [(n, n ^ 1) for n in range(64)])
    same_core = [sorted(range(core, 64, 2), key=place_of) for core in range(2)]
    parts = lax.all_to_all(keep, "vir", 0, 0, axis_index_groups=same_core, tiled=True)
    return jnp.transpose(finish(parts, index))


def solution(mesh):
    specs = (P("occ", "vir"), P(), P(None, "vir", "occ"), P(), P(), P())
    return jax.shard_map(
        shards, mesh=mesh, in_specs=specs, out_specs=P("occ", "vir"), check_vma=False
    )
```

```python
import functools

import jax
import jax.numpy as jnp
from jax import lax
from jax.experimental import pallas as pl
from jax.experimental.pallas import tpu as pltpu
from jax.sharding import PartitionSpec as P

NO = 40
NV = 480
SPAN = 256
IRREPS = 8
RUN_V = 120
RUN_O = 10
ROWS_I = 5
COLS = 32
CD = 3600
SLOTS = 8
LEAD = 256
WIDE = 33 * 128
MAIN = 28 * 128
GROUP = 50
PACK = 2 * SLOTS * RUN_V
ALL_VMEM = 64 * 1024 * 1024
SOME_VMEM = 12 * 1024 * 1024
FULL = 7 * 128
HALF = 64

OCC_ORDER = (0, 5, 2, 7, 4, 1, 6, 3)


def placed():
    return lax.axis_index("occ"), lax.axis_index("vir")


def fill_starts(labels, length, starts):
    bit = 1
    while bit * 2 <= length:
        bit *= 2
    low = [jnp.int32(0)] * IRREPS
    while bit:
        for g in range(1, IRREPS):
            cand = low[g] + bit
            below = labels[jnp.minimum(cand, length) - 1] < g
            low[g] = jnp.where(below, cand, low[g])
        bit //= 2
    for g in range(IRREPS):
        starts[g] = low[g]
    starts[IRREPS] = jnp.int32(length)
    return low


def irrep_of(index, low):
    total = jnp.zeros_like(index)
    for g in range(1, IRREPS):
        total += (index >= low[g]).astype(jnp.int32)
    return total


def turn(near, far, position, inner, lanes):
    shift = position & 127
    amount = (inner + 128 - shift) & 127
    return pltpu.roll(jnp.where(lanes >= shift, near, far), amount, axis=1)


def inner_of(slot):
    return slot * RUN_V % 128


def tiles_of(turned, lanes):
    for slot in range(SLOTS - 1):
        yield jnp.where(lanes < inner_of(slot + 1), turned[slot], turned[slot + 1])
    yield turned[SLOTS - 1]


def first_pair(v):
    return (v * 15) >> 1, (v & 1) * (NV // 2)


def pack_kernel(where_am_i, vir_hbm, int_hbm, out_hbm, labels, starts, ints, whole, packed, sems):
    label_copy = pltpu.make_async_copy(vir_hbm, labels, sems.at[0])
    label_copy.start()
    copies = []
    for s in range(2):
        copies.append(
            [
                pltpu.make_async_copy(int_hbm.at[s], whole.at[s], sems.at[2 + 2 * s]),
            ]
        )
        for copy in copies[s]:
            copy.start()
    o, v = where_am_i()
    c_first, offset = first_pair(v)
    rest = WIDE - LEAD - MAIN - 128
    ints[:, :, pl.ds(0, LEAD)] = jnp.zeros((2, COLS, LEAD), jnp.float32)
    ints[:, :, pl.ds(LEAD + MAIN, 128)] = jnp.zeros((2, COLS, 128), jnp.float32)
    ints[:, :, pl.ds(LEAD + MAIN + 128, rest)] = jnp.zeros((2, COLS, rest), jnp.float32)
    label_copy.wait()
    low = fill_starts(labels, NV, starts)

    lanes = lax.broadcasted_iota(jnp.int32, (COLS, 128), 1)
    row = lax.broadcasted_iota(jnp.int32, (COLS, 128), 0)
    sends = []

    def send(at, size):
        for n in range(8):
            copy = pltpu.make_async_copy(
                packed.at[:, pl.ds(at, size)],
                out_hbm.at[n, :, pl.ds(at, size)],
                sems.at[5 + len(sends)],
            )
            copy.start()
            sends.append(copy)

    held = None
    irr_c = [labels[c_first + slot] for slot in range(SLOTS)]
    begin = [LEAD - offset + low[g] for g in range(IRREPS)]
    for s in range(2):
        for copy in copies[s]:
            copy.wait()
        ints[s, :, pl.ds(LEAD, CD)] = whole[s]
        first = s * SPAN + o * COLS
        a = (first >= NV).astype(jnp.int32)
        b = first - a * NV
        irr_a = labels[a]
        irr_b = irrep_of(row + b, low)
        turned = []
        for slot in range(SLOTS):
            cross = irr_c[slot] ^ irr_a
            mine = irr_b ^ cross
            value = jnp.zeros((COLS, 128), jnp.float32)
            for g in range(IRREPS):
                position = begin[g] + slot * NV
                base = pl.multiple_of(position & -128, 128)
                near = ints[s, :, pl.ds(base, 128)]
                far = ints[s, :, pl.ds(base + 128, 128)]
                moved = turn(near, far, position, inner_of(slot), lanes)
                value = jnp.where(mine == g, moved, value)
            turned.append(value)
            at = s * (FULL + 128)
            if slot:
                tile = jnp.where(lanes < inner_of(slot), turned[slot - 1], value)
                packed[:, pl.ds(at + (slot - 1) * 128, 128)] = tile
            if s == 1 and slot == 4:
                send(FULL + 128, 4 * 128)
        if s == 0:
            held = turned[7]
            send(0, FULL)
        else:
            packed[:, pl.ds(FULL, 128)] = jnp.where(
                lanes < HALF, held, pltpu.roll(turned[7], HALF, axis=1)
            )
            send(FULL, 128)
            send(FULL + 5 * 128, 3 * 128)
    for copy in sends:
        copy.wait()


def pack(where_am_i, integrals_t, vir_irrep):
    anywhere = pl.BlockSpec(memory_space=pl.ANY)
    return pl.pallas_call(
        functools.partial(pack_kernel, where_am_i),
        in_specs=[anywhere, anywhere],
        out_specs=anywhere,
        out_shape=jax.ShapeDtypeStruct((8, COLS, PACK), jnp.float32),
        scratch_shapes=[
            pltpu.SMEM((NV,), jnp.int32),
            pltpu.SMEM((IRREPS + 1,), jnp.int32),
            pltpu.VMEM((2, COLS, WIDE), jnp.float32),
            pltpu.VMEM((2, COLS, CD), jnp.float32),
            pltpu.VMEM((COLS, PACK), jnp.float32),
            pltpu.SemaphoreType.DMA((5 + 32,)),
        ],
        compiler_params=pltpu.CompilerParams(vmem_limit_bytes=ALL_VMEM),
        name="pack",
    )(vir_irrep, integrals_t)


def pack_tau(o, v, vir_ref, occ_ref, vstart, ostart, amp_ref, singles_ref, amps, ones, single_win, left, group, high, low):
    c_first, offset = first_pair(v)
    for t in range(CD // 128 + 1):
        size = min(128, CD - t * 128)
        amps[LEAD // 128 + t, pl.ds(0, ROWS_I * NO), pl.ds(0, size)] = amp_ref[:, pl.ds(t * 128, size)]
    amps[:, pl.ds(ROWS_I * NO, 16), :] = jnp.zeros((WIDE // 128, 16, 128), jnp.float32)

    ones[...] = jnp.zeros_like(ones)
    for t in range(4):
        size = min(128, NV - t * 128)
        ones[t, pl.ds(0, NO), pl.ds(0, size)] = singles_ref[:, pl.ds(t * 128, size)]
    lanes_w = lax.broadcasted_iota(jnp.int32, (16, 128), 1)
    for g in range(IRREPS):
        at, rows = vstart[g], pl.ds(ostart[g], 16)
        single_win[g] = turn(ones[at >> 7, rows, :], ones[(at >> 7) + 1, rows, :], at, 0, lanes_w)
    lane_c = lax.broadcasted_iota(jnp.int32, (8, 128), 1)
    row_i = lax.broadcasted_iota(jnp.int32, (8, 1), 0)
    irr_i = [occ_ref[o * ROWS_I + i] for i in range(ROWS_I)]
    for slot in range(SLOTS):
        c = c_first + slot
        irr_c = vir_ref[c]
        own = ones[c >> 7, pl.ds(o * ROWS_I, 8), :]
        column = jnp.sum(jnp.where(lane_c == (c & 127), own, 0.0), axis=1, keepdims=True)
        for i in range(ROWS_I):
            column = jnp.where((row_i == i) & (irr_i[i] != irr_c), 0.0, column)
        left[slot] = jnp.broadcast_to(column, (8, 128))

    lanes = lax.broadcasted_iota(jnp.int32, (RUN_O, 128), 1)
    for sym in range(IRREPS):
        turned = [[] for _ in range(ROWS_I)]
        for slot in range(SLOTS):
            g = vir_ref[c_first + slot] ^ sym
            begin = slot * NV + vstart[g] - offset
            from_lane = jnp.maximum(0, -begin)
            to_lane = jnp.minimum(vstart[g + 1] - vstart[g], CD - begin)
            inner = inner_of(slot)
            k = (lanes + (128 - inner)) & 127
            keep = (k >= from_lane) & (k < to_lane)
            near = (LEAD + begin) >> 7
            right = pltpu.roll(single_win[g], inner, axis=1)[:RUN_O]
            for i in range(ROWS_I):
                rows = pl.ds(i * NO + ostart[irr_i[i] ^ sym], RUN_O)
                value = turn(amps[near, rows, :], amps[near + 1, rows, :], LEAD + begin, inner, lanes)
                product = left[slot, pl.ds(i, 1), :] * right
                turned[i].append(jnp.where(keep, value + product, 0.0))
        for i in range(ROWS_I):
            for t, tile in enumerate(tiles_of(turned[i], lanes)):
                if t == 7:
                    tile = jnp.where(lanes < HALF, tile, 0.0)
                group[pl.ds(sym * GROUP + i * RUN_O, RUN_O), pl.ds(t * 128, 128)] = tile
    wide = group[:, pl.ds(0, FULL)]
    top = wide.astype(jnp.bfloat16)
    high[:, pl.ds(0, FULL)] = top
    low[...] = (wide - top.astype(jnp.float32)).astype(jnp.bfloat16)
    last = group[:, pl.ds(FULL, 128)]
    upper = last.astype(jnp.bfloat16).astype(jnp.float32)
    lanes_all = lax.broadcasted_iota(jnp.int32, last.shape, 1)
    last = jnp.where(lanes_all < HALF, upper, pltpu.roll(last - upper, HALF, axis=1))
    high[:, pl.ds(FULL, 128)] = last.astype(jnp.bfloat16)


def spread_index(o, u, vir_ref, occ_ref, owner_ref, vlow, olow):
    block = jnp.int32(0)
    for k in range(64):
        block += jnp.where(owner_ref[k] == u, k, 0)
    lanes = lax.broadcasted_iota(jnp.int32, (8, 256), 1)
    row = lax.broadcasted_iota(jnp.int32, (8, 256), 0)
    column = jnp.where(row >= 4, SPAN - 4, 0) + block * 4 + row
    second = column >= NV
    sym = irrep_of(jnp.where(second, column - NV, column), vlow)
    sym = sym ^ jnp.where(second, vir_ref[1], vir_ref[0])
    i = jnp.zeros_like(lanes)
    irr_i = jnp.zeros_like(lanes)
    for n in range(ROWS_I):
        i = jnp.where(lanes >= n * NO, n, i)
        irr_i = jnp.where(lanes >= n * NO, occ_ref[o * ROWS_I + n], irr_i)
    j = lanes - i * NO
    irr_j = irrep_of(j, olow)
    begin = jnp.zeros_like(lanes)
    for g in range(1, IRREPS):
        begin = jnp.where(irr_j == g, olow[g], begin)
    lane = i * RUN_O + j - begin + jnp.where(row >= 4, HALF, 0)
    wanted = ((sym ^ irr_i ^ irr_j) == 0) & (lanes < ROWS_I * NO)
    return jnp.where(wanted, lane, -1)


def tau_kernel(
    where_am_i,
    vir_ref,
    occ_ref,
    owner_ref,
    amp_ref,
    singles_ref,
    high,
    low,
    index_ref,
    vstart,
    ostart,
    amps,
    ones,
    single_win,
    left,
    group,
):
    o, v = where_am_i()
    vlow = fill_starts(vir_ref, NV, vstart)
    olow = fill_starts(occ_ref, NO, ostart)
    pack_tau(o, v, vir_ref, occ_ref, vstart, ostart, amp_ref, singles_ref, amps, ones, single_win, left, group, high, low)
    index_ref[...] = spread_index(o, v, vir_ref, occ_ref, owner_ref, vlow, olow)


def tau(where_am_i, amplitudes, singles, occ_irrep, vir_irrep, owner):
    smem = pl.BlockSpec(memory_space=pltpu.SMEM)
    vmem = pl.BlockSpec(memory_space=pltpu.VMEM)
    depth = SLOTS * 128
    return pl.pallas_call(
        functools.partial(tau_kernel, where_am_i),
        in_specs=[smem, smem, smem, vmem, vmem],
        out_specs=[vmem, vmem, vmem],
        out_shape=[
            jax.ShapeDtypeStruct((IRREPS * GROUP, depth), jnp.bfloat16),
            jax.ShapeDtypeStruct((IRREPS * GROUP, FULL), jnp.bfloat16),
            jax.ShapeDtypeStruct((8, 256), jnp.int32),
        ],
        scratch_shapes=[
            pltpu.SMEM((IRREPS + 1,), jnp.int32),
            pltpu.SMEM((IRREPS + 1,), jnp.int32),
            pltpu.VMEM((WIDE // 128, ROWS_I * NO + 16, 128), jnp.float32),
            pltpu.VMEM((5, NO + 16, 128), jnp.float32),
            pltpu.VMEM((IRREPS, 16, 128), jnp.float32),
            pltpu.VMEM((SLOTS, 8, 128), jnp.float32),
            pltpu.VMEM((IRREPS * GROUP, depth), jnp.float32),
        ],
        compiler_params=pltpu.CompilerParams(vmem_limit_bytes=SOME_VMEM),
        cost_estimate=pl.CostEstimate(flops=0, bytes_accessed=8 * 1024 * 1024, transcendentals=0),
        name="tau",
    )(vir_irrep, occ_irrep, owner, amplitudes, singles)


def place_of(u):
    z = u >> 2
    return ((z & 7) << 2) | ((z >> 3) << 1) | ((u >> 1) & 1)


def ladder_kernel(
    where_am_i, vir_ref, owner_ref, packed_ref, high, low, keep_ref, send_ref, vstart, top, bottom, sums, both_cores
):
    core = where_am_i()[1] & 1
    vlow = fill_starts(vir_ref, NV, vstart)
    lanes = lax.broadcasted_iota(jnp.int32, (COLS, 128), 1)
    contract = functools.partial(
        lax.dot_general,
        dimension_numbers=(((1,), (1,)), ((), ())),
        preferred_element_type=jnp.float32,
    )
    used = IRREPS * GROUP
    sums[pl.ds(used, 8), :] = jnp.zeros((8, 2 * SPAN), jnp.float32)

    def split(s):
        for source in range(8):
            last = packed_ref[source, :, pl.ds(FULL, 128)]
            other = pltpu.roll(last, HALF, axis=1)
            rows = pl.ds(s * SPAN + OCC_ORDER[source] * COLS, COLS)
            wide = packed_ref[source, :, pl.ds(s * (FULL + 128), FULL)]
            upper = wide.astype(jnp.bfloat16)
            top[rows, pl.ds(0, FULL)] = upper
            bottom[rows, pl.ds(0, FULL)] = (wide - upper.astype(jnp.float32)).astype(jnp.bfloat16)
            twice = jnp.where(lanes < HALF, last, other) if s == 0 else jnp.where(lanes < HALF, other, last)
            upper = twice.astype(jnp.bfloat16)
            top[rows, pl.ds(FULL, 128)] = upper
            rest = jnp.where(lanes < HALF, twice - upper.astype(jnp.float32), 0.0)
            bottom[rows, pl.ds(FULL, 128)] = rest.astype(jnp.bfloat16)

    def multiply(s):
        there = pl.ds(s * SPAN, SPAN)
        sums[pl.ds(0, used), there] = (
            contract(high[...], top[there, :])
            + contract(high[...], bottom[there, :])
            + contract(low[...], top[there, pl.ds(0, FULL)])
        )

    def pick(s):
        there = pl.ds(s * SPAN, SPAN)
        column = lax.broadcasted_iota(jnp.int32, (1, SPAN), 1) + s * SPAN
        second = column >= NV
        sym = irrep_of(jnp.where(second, column - NV, column), vlow)
        sym = sym ^ jnp.where(second, vir_ref[1], vir_ref[0])
        picked = sums[pl.ds(0, 56), there]
        for g in range(1, IRREPS):
            picked = jnp.where(sym == g, sums[pl.ds(g * GROUP, 56), there], picked)
        return picked

    split(0)
    multiply(0)
    split(1)
    multiply(1)
    pad = jnp.zeros((HALF - 56, SPAN), jnp.float32)
    both = 0.5 * jnp.transpose(jnp.concatenate([pick(0), pad, pick(1), pad], axis=0))
    for k in range(64):
        u = owner_ref[k]
        both_cores[(u & 1) ^ core, place_of(u)] = both[4 * k : 4 * k + 4, :]
    keep_ref[...] = both_cores[0]
    send_ref[...] = both_cores[1]


def ladder(where_am_i, packed, high, low, vir_irrep, owner):
    smem = pl.BlockSpec(memory_space=pltpu.SMEM)
    vmem = pl.BlockSpec(memory_space=pltpu.VMEM)
    depth = SLOTS * 128
    return pl.pallas_call(
        functools.partial(ladder_kernel, where_am_i),
        in_specs=[smem, smem, vmem, vmem, vmem],
        out_specs=[vmem, vmem],
        out_shape=[jax.ShapeDtypeStruct((32, 4, 128), jnp.float32)] * 2,
        scratch_shapes=[
            pltpu.SMEM((IRREPS + 1,), jnp.int32),
            pltpu.VMEM((2 * SPAN, depth), jnp.bfloat16),
            pltpu.VMEM((2 * SPAN, depth), jnp.bfloat16),
            pltpu.VMEM((IRREPS * GROUP + 8, 2 * SPAN), jnp.float32),
            pltpu.VMEM((2, 32, 4, 128), jnp.float32),
        ],
        compiler_params=pltpu.CompilerParams(vmem_limit_bytes=SOME_VMEM),
        name="ladder",
    )(vir_irrep, owner, packed, high, low)


def finish_kernel(parts_ref, index_ref, out_ref):
    total = jnp.sum(parts_ref[...], axis=0)
    both = jnp.concatenate([total, total], axis=0)
    index = index_ref[...]
    lane = jnp.maximum(index, 0)
    near = jnp.take_along_axis(both, lane[:, :128], axis=1)
    far = jnp.take_along_axis(both, lane[:, 128:], axis=1)
    result = jnp.where(index >= 0, jnp.concatenate([near, far], axis=1), 0.0)
    out_ref[...] = result[:, : ROWS_I * NO]


def finish(parts, index):
    vmem = pl.BlockSpec(memory_space=pltpu.VMEM)
    return pl.pallas_call(
        finish_kernel,
        in_specs=[vmem, vmem],
        out_specs=vmem,
        out_shape=jax.ShapeDtypeStruct((8, ROWS_I * NO), jnp.float32),
        compiler_params=pltpu.CompilerParams(vmem_limit_bytes=1024 * 1024),
        name="finish",
    )(parts, index)


def shards(amplitudes, singles, integrals, occ_irrep, vir_irrep, owner):
    packed = pack(placed, jnp.transpose(integrals, (0, 2, 1)), vir_irrep)
    gathered = lax.all_to_all(
        packed, "occ", 0, 0, axis_index_groups=[list(OCC_ORDER)], tiled=True
    )
    high, low, index = tau(placed, amplitudes, singles, occ_irrep, vir_irrep, owner)
    keep, send = ladder(placed, gathered, high, low, vir_irrep, owner)
    keep += lax.ppermute(send, "vir", [(n, n ^ 1) for n in range(64)])
    same_core = [sorted(range(core, 64, 2), key=place_of) for core in range(2)]
    parts = lax.all_to_all(keep, "vir", 0, 0, axis_index_groups=same_core, tiled=True)
    return jnp.transpose(finish(parts, index))


def solution(mesh):
    specs = (P("occ", "vir"), P(), P(None, "vir", "occ"), P(), P(), P())
    return jax.shard_map(
        shards, mesh=mesh, in_specs=specs, out_specs=P("occ", "vir"), check_vma=False
    )
```
